128 devices in a mesh: dp: 16 (over z, x), fsdp: 8 (over y, core).
Axes of the slice: x: 4, y: 4, z: 4, core: 2. Of those that a mesh axis runs over, the one named last changes fastest.
Arguments:
- tokens: bfloat16 [65536, 4096], P(('dp', 'fsdp')), may hold values from -80 to 80
- cotangent: bfloat16 [65536, 768], P(('dp', 'fsdp')), may hold values from -6 to 6
- old_weight: bfloat16 [128, 8, 5, 1536], P(('dp', 'fsdp')), may hold values from -0.08984375 to 0.08984375
- old_first: float32 [128, 8, 5, 1536], P(('dp', 'fsdp')), may hold values from -2 to 2
- old_second: float32 [128, 8, 5, 1536], P(('dp', 'fsdp')), may hold values from 0.05 to 1
- old_holder: int32 [4096, 1], replicated, may hold values from 0 to 127; in each aligned block of 512 rows (0 to 511, 512 to 1023, ...) at most 5 rows name the same one
- new_owner: int32 [4096, 1], replicated, may hold values from 0 to 15; in each aligned block of 512 rows (0 to 511, 512 to 1023, ...) at most 48 rows name the same one
Outputs:
- input_grad: bfloat16 [65536, 4096], P(('dp', 'fsdp'))
- new_weight: bfloat16 [4096, 1536], P('fsdp')
- new_first: float32 [8, 16, 48, 1536], P('fsdp', 'dp')
- new_second: float32 [8, 16, 48, 1536], P('fsdp', 'dp')
The draws below stay inside these ranges and needn't reach their ends.
Inputs may be any that keep to these rules, and one draw needn't show every extreme that they name: `old_holder`: among the rows of any one shard (aligned blocks of 512 rows), no device holds more than 5; some device holds exactly 5. `new_owner`: among the rows of any one shard (aligned blocks of 512 rows), no replica owns more than 48; some replica owns exactly 48.
All inputs are finite; a program needn't handle non-finite values.
Results may differ from the reference program's by a relative error of at most 0.013.
Values may be sent and summed in bfloat16 or wider, within the bound.
No kernel may reach another device: no remote copies, remote signals or barrier semaphores. Data moves between devices by JAX's collectives and lax.ppermute only.
A program may use at most 128 MiB of HBM per device.

```python
import math
import jax
import jax.numpy as jnp
import numpy as np
from jax import lax

D = 4096
FF = 768
TOK_DEV = 512
TOKENS = 65536
SHARD = 512
HOLD = 5
OWN = 48
N_DP = 16
N_FSDP = 8
DEVICES = 128


def draw_tokens(key, part):
    key = jax.random.fold_in(key, 11)
    noise_key, jitter_key = jax.random.split(key, 2)
    position = jnp.arange(D, dtype=jnp.float32) / D
    column_scale = jnp.exp(math.log(10.0) * position) * jax.random.uniform(jitter_key, (D,), jnp.float32, 0.7, 1.3)
    normals = jnp.clip(jax.random.normal(noise_key, (TOKENS, D), jnp.float32), -6.0, 6.0)
    values = normals * column_scale
    return values.astype(jnp.bfloat16)


def block_levels(own_key, dims, cuts, low, top_value):
    gain = 1.0
    for axis_at, blocks in cuts:
        steps = jax.random.uniform(jax.random.fold_in(jax.random.fold_in(own_key, 6), axis_at), (blocks,), jnp.float32, low / len(cuts), top_value / len(cuts))
        gain = gain * jnp.repeat(jnp.exp(steps), dims[axis_at] // blocks).reshape((-1,) + (1,) * (len(dims) - 1 - axis_at))
    return gain


def deal_out(stream_key, own, number, rows, count, top, reach, slope):
    order = jax.random.permutation(stream_key, count)
    heavy_load, common = shares(count, rows * top, reach, slope, True), shares(count, rows * top, reach, slope, False)
    places = jnp.arange(count)

    def named(lengths, offset_by):
        used = int((lengths > 0).sum())
        fixed = max(1, used // 4)
        shifted = fixed + (places - fixed + offset_by * (used - fixed)) % max(1, count - fixed)
        return jnp.zeros((count,), jnp.int32).at[order[jnp.where(places < fixed, places, shifted)]].set(jnp.asarray(lengths, jnp.int32))

    lengths = jnp.where(number % 4 == 0, named(heavy_load, number // 4), named(common, number - number // 4 - 1))
    mixed = jax.random.permutation(jax.random.fold_in(own, 3), count)
    source_of, sink = mixed[0:count // 2 * 2:2], mixed[1:count // 2 * 2:2]
    room = jnp.minimum(lengths[source_of] - 1, reach - lengths[sink]) // 2
    room = jnp.where((source_of == order[0]) | (sink == order[0]) | (lengths[sink] == 0), 0, jnp.maximum(room, 0))
    shifted = jax.random.randint(jax.random.fold_in(own, 4), (count // 2,), 0, 1 << 20) % (room + 1)
    lengths = lengths.at[source_of].add(-shifted).at[sink].add(shifted)
    members = jnp.searchsorted(jnp.cumsum(lengths), jnp.arange(rows * top), side="right").astype(jnp.int32)
    table = members.reshape(top, rows).T
    table = table[jax.random.permutation(jax.random.fold_in(own, 1), rows)]
    offset_by = jax.random.randint(jax.random.fold_in(own, 2), (rows, 1), 0, top)
    return jnp.take_along_axis(table, (jnp.arange(top)[None, :] + offset_by) % top, axis=1)


def shares(amount, total, most, lean, full):
    loads = [(1 << 20) // math.isqrt(standing ** lean) + 1 for standing in range(1, amount + 1)]
    largest = most if full else min(most, max(-(-total // amount), total * loads[0] // sum(loads)))
    least = 1 if total - largest >= amount - 1 else 0
    holding, rest = [largest] + [least] * (amount - 1), total - largest - least * (amount - 1)
    while rest > 0:
        movable = [i for i in range(1, amount) if holding[i] < largest] or [i for i in range(1, amount) if holding[i] < most]
        mass, left = sum([loads[i] for i in movable]), rest
        for i in movable:
            addition = min(most - holding[i], max(1, left * loads[i] // mass), rest)
            holding[i] = holding[i] + addition
            rest = rest - addition
    return np.array(holding)


def bell_draw(stream_key, extent, width, limit, cuts=(), kind=jnp.bfloat16):
    array = jax.random.normal(stream_key, extent, jnp.float32) * width
    if len(cuts) > 0:
        array = block_levels(stream_key, extent, cuts, -0.22, 0.18) * array
    return jnp.clip(array, min=-limit, max=limit).astype(kind)


def setup_inputs(seed: int = 0) -> dict:
    key_list = jax.random.split(jax.random.key(seed), 8)
    tokens = draw_tokens(jax.random.fold_in(key_list[7], 71), 0)
    cotangent = bell_draw(key_list[1], (TOKENS, FF), 1.0, 6.0, ((0, 128),))
    old_weight = bell_draw(key_list[2], (DEVICES, N_FSDP, HOLD, 2 * FF), 0.015, 0.08984375, ((0, 128),))
    old_first = bell_draw(key_list[3], (DEVICES, N_FSDP, HOLD, 2 * FF), 0.3, 2.0, ((0, 128),), jnp.float32)
    old_second = jnp.clip(jnp.exp(math.log(1.0) - 2.9957323 * jax.random.uniform(key_list[4], (DEVICES, N_FSDP, HOLD, 2 * FF), jnp.float32) ** block_levels(key_list[4], (DEVICES, N_FSDP, HOLD, 2 * FF), ((0, 128),), -0.2, 0.2)), 0.05, 1.0)
    old_holder_keys = jax.random.split(jax.random.fold_in(key_list[5], 1), D // SHARD)
    old_holder_turns = jax.random.permutation(jax.random.fold_in(key_list[5], 3), D // SHARD)
    old_holder = jax.vmap(lambda own, number: deal_out(jax.random.fold_in(key_list[5], 2), own, number, SHARD, DEVICES, 1, HOLD, 1))(old_holder_keys, old_holder_turns).reshape((D, 1))
    new_owner_keys = jax.random.split(jax.random.fold_in(key_list[6], 1), D // SHARD)
    new_owner_turns = jax.random.permutation(jax.random.fold_in(key_list[6], 3), D // SHARD)
    new_owner = jax.vmap(lambda own, number: deal_out(jax.random.fold_in(key_list[6], 2), own, number, SHARD, N_DP, 1, OWN, 2))(new_owner_keys, new_owner_turns).reshape((D, 1))
    return {"tokens": tokens, "cotangent": cotangent, "old_weight": old_weight, "old_first": old_first, "old_second": old_second, "old_holder": old_holder, "new_owner": new_owner}


beta_one = 0.9
beta_two = 0.999
learn_rate = 0.01
adam_eps = 1e-08
step_count = 100

def rank_within(labels, classes):
    matches = (labels[..., None] == jnp.arange(classes, dtype=jnp.int32)).astype(jnp.int32)
    running = jnp.cumsum(matches, axis=-2)
    return (lax.optimization_barrier(jnp.sum(running * matches, axis=-1)) - 1).astype(jnp.int32)

def hidden_grad(gate_up, cotangent):
    half_width = gate_up.shape[1] // 2
    gate_part = gate_up[:, :half_width]
    up_part = gate_up[:, half_width:]
    sigmoid_gate = jax.nn.sigmoid(gate_part)
    upstream = cotangent.astype(jnp.float32)
    d_gate = upstream * up_part * sigmoid_gate * (1.0 + gate_part * (1.0 - sigmoid_gate))
    d_up = upstream * gate_part * sigmoid_gate
    return jnp.concatenate([d_gate, d_up], axis=1).astype(jnp.bfloat16)

def reference(tokens, cotangent, old_weight, old_first, old_second, old_holder, new_owner):
    row_width = 2 * FF
    row_ids = jnp.arange(D, dtype=jnp.int32)
    holder = old_holder[:, 0].astype(jnp.int32)
    held_rank = rank_within(holder.reshape(N_FSDP, SHARD), DEVICES).reshape(D)
    source = holder * (N_FSDP * HOLD) + row_ids // SHARD * HOLD + held_rank
    weight = jnp.take(old_weight.reshape(-1, row_width), source, axis=0)
    first_rows = jnp.take(old_first.reshape(-1, row_width), source, axis=0)
    second_rows = jnp.take(old_second.reshape(-1, row_width), source, axis=0)

    def per_device(accum_sum, device_block):
        x_block, cot_block = device_block
        gate_up = jnp.dot(x_block, weight, preferred_element_type=jnp.float32)
        dmixed = hidden_grad(gate_up, cot_block)
        back_grad = jnp.dot(dmixed, weight.T, preferred_element_type=jnp.float32).astype(jnp.bfloat16)
        partial_sum = lax.dot_general(x_block, dmixed, (((0,), (0,)), ((), ())), preferred_element_type=jnp.float32)
        rounded = lax.optimization_barrier(partial_sum.astype(jnp.bfloat16))
        return (accum_sum + rounded.astype(jnp.float32), back_grad)
    blocks = (tokens.reshape(DEVICES, TOK_DEV, D), cotangent.reshape(DEVICES, TOK_DEV, FF))
    grad_sum, back_grad = lax.scan(per_device, jnp.zeros((D, row_width), jnp.float32), blocks)
    input_grad = back_grad.reshape(TOKENS, D)
    total_sq = jnp.sum(grad_sum * grad_sum)
    clip_norm = math.sqrt(D * row_width)
    factor = jnp.minimum(1.0, clip_norm / jnp.sqrt(total_sq + 1e-06))
    clipped = grad_sum * factor
    first_next = beta_one * first_rows + (1.0 - beta_one) * clipped
    second_next = beta_two * second_rows + (1.0 - beta_two) * clipped * clipped
    bias_one = 1.0 - beta_one ** step_count
    bias_two = 1.0 - beta_two ** step_count
    update = learn_rate * (first_next / bias_one) / (jnp.sqrt(second_next / bias_two) + adam_eps)
    new_weight = (weight.astype(jnp.float32) - update).astype(jnp.bfloat16)
    owner_dp = new_owner[:, 0].astype(jnp.int32).reshape(N_FSDP, SHARD)
    own_rank = rank_within(owner_dp, N_DP)
    picked = (owner_dp[:, :, None, None] == jnp.arange(N_DP, dtype=jnp.int32)[None, None, :, None]) & (own_rank[:, :, None, None] == jnp.arange(OWN, dtype=jnp.int32)[None, None, None, :])
    row_grid = row_ids.reshape(N_FSDP, SHARD)
    slot_rows = lax.optimization_barrier(jnp.sum(jnp.where(picked, row_grid[:, :, None, None], 0), axis=1)).astype(jnp.int32)
    filled = jnp.any(picked, axis=1)
    new_first = jnp.where(filled[..., None], jnp.take(first_next, slot_rows, axis=0), 0.0)
    new_second = jnp.where(filled[..., None], jnp.take(second_next, slot_rows, axis=0), 0.0)
    return (input_grad, new_weight, new_first, new_second)
```

```python
import math

import jax
import jax.numpy as jnp
from jax import lax
from jax.experimental import pallas as pl
from jax.experimental.pallas import tpu as pltpu
from jax.sharding import PartitionSpec as P

beta_one = 0.9
beta_two = 0.999
learn_rate = 0.01
adam_eps = 1e-08
step_count = 100

AXES = ("dp", "fsdp")
SIZE = {"z": 4, "x": 4, "y": 4, "c": 2}
GATHER_ORDER = (("z", "x", "y"), ("x", "y", "z"), ("y", "z", "x"))
REDUCE_ORDER = (("y", "z", "x"), ("z", "y", "x"), ("x", "y", "z"))
SHIFTS = (1, 3, 2)
SLOTS = 5


def device_id(place):
    return ((place["z"] * 4 + place["x"]) * 4 + place["y"]) * 2 + place["c"]


def shift_pairs(axis, shift):
    pairs = []
    for z in range(4):
        for x in range(4):
            for y in range(4):
                for c in range(2):
                    place = {"z": z, "x": x, "y": y, "c": c}
                    target = dict(place)
                    target[axis] = (place[axis] + shift) % SIZE[axis]
                    pairs.append((device_id(place), device_id(target)))
    return pairs


def send(value, axis, shift):
    return lax.ppermute(value, AXES, shift_pairs(axis, shift))


def my_place():
    dp_at = lax.axis_index("dp")
    fsdp_at = lax.axis_index("fsdp")
    return {"z": dp_at // 4, "x": dp_at % 4, "y": fsdp_at // 2, "c": fsdp_at % 2}


def relative(source, mine):
    away = (source - mine) % 4
    return jnp.where(away == 0, 0, jnp.where(away == 3, 1, jnp.where(away == 1, 2, 3)))


def gather_axis(block, axis):
    return [block] + [send(block, axis, shift) for shift in SHIFTS]


def symmetric_sum(parts):
    own, left, right, across = [part.astype(jnp.float32) for part in parts]
    return (own + across) + (left + right)


def forward_kernel(index_ref, own_ref, other_ref, *refs):
    slot_refs = refs[:12]
    own_cot_ref, other_cot_ref, weight_ref, dmixed_ref, acc_ref, slots_ref = refs[12:]
    step = pl.program_id(0)

    @pl.when(step == 0)
    def _():
        acc_ref[...] = jnp.zeros_like(acc_ref)

    for group in range(3):
        for piece in range(4):
            slots_ref[group, piece * 160 : (piece + 1) * 160, :] = slot_refs[group * 4 + piece][0]
    lanes = lax.broadcasted_iota(jnp.int32, (512, 640), 1)
    for group in range(3):
        pick = (index_ref[:, group : group + 1] == lanes).astype(jnp.bfloat16)
        rows = jnp.dot(pick, slots_ref[group], preferred_element_type=jnp.float32)
        weight_ref[:, group * 256 : (group + 1) * 256] = rows.astype(jnp.bfloat16)
    acc_ref[:512, :] += jnp.dot(own_ref[...], weight_ref[...], preferred_element_type=jnp.float32)
    acc_ref[512:, :] += jnp.dot(other_ref[...], weight_ref[...], preferred_element_type=jnp.float32)

    @pl.when(step == pl.num_programs(0) - 1)
    def _():
        for half, cot_ref in enumerate((own_cot_ref, other_cot_ref)):
            rows = slice(half * 512, half * 512 + 512)
            for group in range(3):
                at = group * 256
                gate = acc_ref[rows, at : at + 128]
                up = acc_ref[rows, at + 128 : at + 256]
                cot = cot_ref[:, group * 128 : (group + 1) * 128].astype(jnp.float32)
                sig = 1.0 / (1.0 + jnp.exp(-gate))
                d_gate = cot * up * sig * (1.0 + gate * (1.0 - sig))
                d_up = cot * gate * sig
                dmixed_ref[rows, at : at + 128] = d_gate.astype(jnp.bfloat16)
                dmixed_ref[rows, at + 128 : at + 256] = d_up.astype(jnp.bfloat16)


def forward(index, own, other, slots, own_cot, other_cot):
    tokens_spec = pl.BlockSpec((512, 512), lambda b: (0, b))
    return pl.pallas_call(
        forward_kernel,
        grid=(8,),
        in_specs=[pl.BlockSpec((512, 8), lambda b: (b, 0)), tokens_spec, tokens_spec]
        + [pl.BlockSpec((1, 160, 256), lambda b: (b, 0, 0))] * 12
        + [pl.BlockSpec((512, 384), lambda b: (0, 0))] * 2,
        out_specs=[
            pl.BlockSpec((512, 768), lambda b: (b, 0)),
            pl.BlockSpec((1024, 768), lambda b: (0, 0)),
        ],
        out_shape=[
            jax.ShapeDtypeStruct((4096, 768), jnp.bfloat16),
            jax.ShapeDtypeStruct((1024, 768), jnp.bfloat16),
        ],
        scratch_shapes=[
            pltpu.VMEM((1024, 768), jnp.float32),
            pltpu.VMEM((3, 640, 256), jnp.bfloat16),
        ],
        compiler_params=pltpu.CompilerParams(vmem_limit_bytes=40 * 1024 * 1024),
        cost_estimate=pl.CostEstimate(
            flops=2 * (1024 * 4096 * 768 + 4096 * 640 * 768), bytes_accessed=26_000_000, transcendentals=400_000
        ),
    )(index, own, other, *slots, own_cot, other_cot)


def on_device(tokens, cotangent, old_weight, old_first, old_second, old_holder, new_owner):
    me = my_place()
    core = me["c"]
    dp_at = lax.axis_index("dp")
    fsdp_at = lax.axis_index("fsdp")

    holder = old_holder[:, 0].reshape(8, 512)
    order = jnp.arange(512, dtype=jnp.int32)
    before = order[None, :] < order[:, None]
    held_rank = jnp.sum(
        ((holder[:, None, :] == holder[:, :, None]) & before[None]).astype(jnp.int32), axis=2
    )
    source = {"z": holder // 32, "x": holder // 8 % 4, "y": holder // 2 % 4, "c": holder % 2}
    rel = {axis: relative(source[axis], me[axis]) for axis in "zxy"}
    rel_core = (source["c"] != core).astype(jnp.int32)
    index = jnp.stack(
        [
            rel[third] * 160 + rel[second] * 40 + rel[first] * 10 + rel_core * 5 + held_rank
            for first, second, third in GATHER_ORDER
        ],
        axis=-1,
    ).reshape(4096, 3)
    index = jnp.pad(index, ((0, 0), (0, 5)))

    by_half = old_weight[0].reshape(8, SLOTS, 2, 2, 3, 128).transpose(3, 4, 0, 1, 2, 5).reshape(2, 3, 8, SLOTS, 256)
    kept = lax.dynamic_index_in_dim(by_half, core, 0, keepdims=False)
    given = lax.dynamic_index_in_dim(by_half, 1 - core, 0, keepdims=False)
    got = send(given, "c", 1)
    slots = []
    both = jnp.concatenate([kept, got], axis=2)
    blocks = [both[group] for group in range(3)]
    for stage in range(2):
        parts = [gather_axis(blocks[group], GATHER_ORDER[group][stage]) for group in range(3)]
        blocks = [jnp.concatenate(part, axis=1) for part in parts]
    parts = [gather_axis(blocks[group], GATHER_ORDER[group][2]) for group in range(3)]
    slots = [piece for part in parts for piece in part]

    other_tokens = send(tokens, "c", 1)
    cot_half = cotangent.reshape(512, 2, 384)
    own_cot = lax.dynamic_index_in_dim(cot_half, core, 1, keepdims=False)
    other_cot = send(lax.dynamic_index_in_dim(cot_half, 1 - core, 1, keepdims=False), "c", 1)

    weight, dmixed = forward(index, tokens, other_tokens, slots, own_cot, other_cot)

    pair = jnp.concatenate([tokens, other_tokens], axis=0)
    grads = [
        lax.dot_general(
            pair,
            dmixed[:, group * 256 : (group + 1) * 256],
            (((0,), (0,)), ((), ())),
            preferred_element_type=jnp.float32,
        ).astype(jnp.bfloat16)
        for group in range(3)
    ]
    late = lax.optimization_barrier((dmixed, weight, *grads))
    dmixed_late, weight_late = late[0], late[1]

    moments = jnp.concatenate([old_first[0].astype(jnp.bfloat16), old_second[0].astype(jnp.bfloat16)], axis=1)
    moments = moments.reshape(4, 2, 2 * SLOTS, 1536)
    mine = lax.dynamic_index_in_dim(moments, core, 1, keepdims=False)
    theirs = lax.dynamic_index_in_dim(moments, 1 - core, 1, keepdims=False)
    chip = jnp.concatenate([mine, send(theirs, "c", 1)], axis=1)

    def for_y(shift):
        return lax.dynamic_index_in_dim(chip, (me["y"] + shift) % 4, 0, keepdims=False)

    shard_moments = jnp.concatenate([for_y(0)] + [send(for_y(shift), "y", shift) for shift in SHIFTS], axis=0)
    all_moments = lax.all_gather(shard_moments, "dp", axis=0, tiled=True)
    my_holder = lax.dynamic_index_in_dim(holder, fsdp_at, 0, keepdims=False)
    my_rank = lax.dynamic_index_in_dim(held_rank, fsdp_at, 0, keepdims=False)
    moment_at = (
        my_holder // 8 * 80
        + relative(my_holder // 2 % 4, me["y"]) * 20
        + (my_holder % 2 != core).astype(jnp.int32) * 10
        + my_rank
    )
    first_rows = jnp.take(all_moments, moment_at, axis=0)
    second_rows = jnp.take(all_moments, moment_at + SLOTS, axis=0)
    owner = lax.dynamic_index_in_dim(new_owner[:, 0].reshape(8, 512), fsdp_at, 0, keepdims=False)
    own_rank = jnp.sum(((owner[None, :] == owner[:, None]) & before).astype(jnp.int32), axis=1)
    picked = (owner == dp_at)[None, :] & (own_rank[None, :] == jnp.arange(48, dtype=jnp.int32)[:, None])
    my_rows = jnp.sum(jnp.where(picked, order[None, :], 0), axis=1)
    my_fill = jnp.any(picked, axis=1)[:, None]
    first_own = jnp.take(first_rows, my_rows, axis=0)
    second_own = jnp.take(second_rows, my_rows, axis=0)

    def take_chunk(value, axis_at, at):
        return lax.dynamic_index_in_dim(value, at % 4, axis_at, keepdims=False)

    finals = []
    for group in range(3):
        first_axis, second_axis, third_axis = REDUCE_ORDER[group]
        value = grads[group].reshape(4, 2, 4, 4, 32, 256)
        names = ["y", "s", "z", "x"]
        for axis in (first_axis, second_axis):
            dim = names.index(axis)
            parts = [take_chunk(value, dim, me[axis])]
            parts += [send(take_chunk(value, dim, me[axis] + shift), axis, shift) for shift in SHIFTS]
            value = symmetric_sum(parts).astype(jnp.bfloat16)
            names.remove(axis)
        keep = lax.dynamic_index_in_dim(value, core, 0, keepdims=False)
        give = lax.dynamic_index_in_dim(value, 1 - core, 0, keepdims=False)
        recv = send(give, "c", 1)
        low = jnp.where(core == 0, keep, recv)
        high = jnp.where(core == 0, recv, keep)
        value = jnp.concatenate([low, high], axis=-1)
        value = symmetric_sum(gather_axis(value, third_axis)).astype(jnp.bfloat16)
        split_axis = "x" if third_axis == "z" else "z"
        parts = gather_axis(value, split_axis)
        stacked = jnp.stack(parts)
        spots = (jnp.arange(4, dtype=jnp.int32) - me[split_axis]) % 4
        lookup = relative(jnp.arange(4, dtype=jnp.int32), me[split_axis])
        stacked = jnp.take(stacked, lookup, axis=0)
        if split_axis == "x":
            stacked = stacked.transpose(1, 0, 2, 3)
        finals.append(stacked.reshape(512, 2, 2, 128))
    summed = jnp.stack(finals, axis=2).transpose(0, 3, 1, 2, 4).reshape(512, 1536).astype(jnp.float32)

    local_sq = jnp.broadcast_to(jnp.sum(summed * summed), (8, 128))
    chip_sq = local_sq + send(local_sq, "c", 1)
    total_sq = symmetric_sum(gather_axis(chip_sq, "y"))[0, 0]
    clip_norm = math.sqrt(4096 * 1536)
    factor = jnp.minimum(1.0, clip_norm / jnp.sqrt(total_sq + 1e-06))
    bias_one = 1.0 - beta_one**step_count
    bias_two = 1.0 - beta_two**step_count

    def moments_next(grad, first, second):
        clipped = grad * factor
        first_next = beta_one * first.astype(jnp.float32) + (1.0 - beta_one) * clipped
        second_next = beta_two * second.astype(jnp.float32) + (1.0 - beta_two) * clipped * clipped
        return first_next, second_next

    shard_weights = lax.dynamic_slice_in_dim(weight_late, me["y"] * 1024, 1024, 0).reshape(2, 512, 768)
    keep = lax.dynamic_index_in_dim(shard_weights, core, 0, keepdims=False)
    recv = send(lax.dynamic_index_in_dim(shard_weights, 1 - core, 0, keepdims=False), "c", 1)
    low = jnp.where(core == 0, keep, recv).reshape(512, 3, 2, 128)
    high = jnp.where(core == 0, recv, keep).reshape(512, 3, 2, 128)
    shard_w = jnp.stack([low, high], axis=1).transpose(0, 3, 1, 2, 4).reshape(512, 1536)

    first_next, second_next = moments_next(summed, first_rows, second_rows)
    update = learn_rate * (first_next / bias_one) / (jnp.sqrt(second_next / bias_two) + adam_eps)
    new_shard = (shard_w.astype(jnp.float32) - update).astype(jnp.bfloat16)
    grad_own = jnp.take(summed, my_rows, axis=0)
    first_out, second_out = moments_next(grad_own, first_own, second_own)
    first_out = jnp.where(my_fill, first_out, 0.0)
    second_out = jnp.where(my_fill, second_out, 0.0)

    def back(rows):
        return lax.dot_general(rows, weight_late, (((1,), (1,)), ((), ())), preferred_element_type=jnp.float32)

    partner_part = send(back(dmixed_late[512:]).astype(jnp.bfloat16), "c", 1)
    input_grad = (back(dmixed_late[:512]) + partner_part.astype(jnp.float32)).astype(jnp.bfloat16)
    return (input_grad, new_shard, first_out[None, None], second_out[None, None])


def solution(mesh):
    placed = (
        P(("dp", "fsdp"), None),
        P(("dp", "fsdp"), None),
        P(("dp", "fsdp"), None, None, None),
        P(("dp", "fsdp"), None, None, None),
        P(("dp", "fsdp"), None, None, None),
        P(),
        P(),
    )
    return jax.shard_map(
        on_device,
        mesh=mesh,
        in_specs=placed,
        out_specs=(
            P(("dp", "fsdp"), None),
            P("fsdp", None),
            P("fsdp", "dp", None, None),
            P("fsdp", "dp", None, None),
        ),
        check_vma=False,
    )
```

```python
import math

import jax
import jax.numpy as jnp
import numpy as np
from jax import lax
from jax.experimental import pallas as pl
from jax.experimental.pallas import tpu as pltpu
from jax.sharding import Mesh
from jax.sharding import PartitionSpec as P

beta_one = 0.9
beta_two = 0.999
learn_rate = 0.01
adam_eps = 1e-08
step_count = 100

SIZE = {"z": 4, "x": 4, "y": 4, "c": 2}
SHIFTS = (1, 3, 2)
OFFSETS = (0, 3, 1, 2)
SLOTS = 5
BF16 = jnp.bfloat16
F32 = jnp.float32


def send(value, axis, shift):
    size = SIZE[axis]
    return lax.ppermute(value, axis, [(i, (i + shift) % size) for i in range(size)])


def gather_axis(block, axis):
    return [block] + [send(block, axis, shift) for shift in SHIFTS]


def relative(source, mine):
    away = (source - mine) % 4
    return jnp.where(away == 0, 0, jnp.where(away == 3, 1, jnp.where(away == 1, 2, 3)))


def symmetric_sum(parts):
    own, left, right, across = [part.astype(F32) for part in parts]
    return (own + across) + (left + right)


def pick_rows(index, rows):
    lanes = lax.broadcasted_iota(jnp.int32, (index.shape[0], rows.shape[0]), 1)
    pick = (index == lanes).astype(BF16)
    return jnp.dot(pick, rows, preferred_element_type=F32).astype(BF16)


def params(mib):
    return pltpu.CompilerParams(vmem_limit_bytes=mib * 1024 * 1024)


def cost(macs, moved):
    return pl.CostEstimate(flops=2 * macs, bytes_accessed=moved, transcendentals=0)


def first_merge_source():
    i = np.arange(320)
    b, rel, core, k = i // 40, i // 10 % 4, i // 5 % 2, i % 5
    return (rel * 80 + core * 40 + b * 5 + k).astype(np.int32)[:, None]


def first_merge_kernel(source_ref, a_ref, b_ref, c_ref, d_ref, left_ref, right_ref, rows_ref):
    for piece, ref in enumerate((a_ref, b_ref, c_ref, d_ref)):
        rows_ref[piece * 80 : (piece + 1) * 80, :] = ref[...]
    placed = pick_rows(source_ref[...], rows_ref[...])
    left_ref[...] = placed[:, :256]
    right_ref[...] = placed[:, 256:]


def first_merge(parts):
    return pl.pallas_call(
        first_merge_kernel,
        out_shape=[jax.ShapeDtypeStruct((320, 256), BF16)] * 2,
        scratch_shapes=[pltpu.VMEM((320, 512), BF16)],
        compiler_params=params(16),
        cost_estimate=cost(320 * 320 * 512, 1_000_000),
    )(jnp.asarray(first_merge_source()), *parts)


def second_merge_source():
    i = np.arange(320)
    b, rel, j = i // 160, i // 40 % 4, i % 40
    return (rel * 80 + b * 40 + j).astype(np.int32)[:, None]


def second_merge_kernel(source_ref, a_ref, b_ref, c_ref, d_ref, out_ref, rows_ref):
    for pair in range(4):
        for piece, ref in enumerate((a_ref, b_ref, c_ref, d_ref)):
            rows_ref[piece * 80 : (piece + 1) * 80, :] = ref[pair * 80 : (pair + 1) * 80, :]
        out_ref[pair * 320 : (pair + 1) * 320, :] = pick_rows(source_ref[...], rows_ref[...])


def second_merge(parts):
    return pl.pallas_call(
        second_merge_kernel,
        out_shape=jax.ShapeDtypeStruct((1280, 256), BF16),
        scratch_shapes=[pltpu.VMEM((320, 256), BF16)],
        compiler_params=params(16),
        cost_estimate=cost(4 * 320 * 320 * 256, 1_500_000),
    )(jnp.asarray(second_merge_source()), *parts)


def whole_merge_source():
    i = np.arange(640)
    b, chip, core, k = i // 80, i // 10 % 8, i // 5 % 2, i % 5
    return (chip * 80 + core * 40 + b * 5 + k).astype(np.int32)[:, None]


def whole_merge_kernel(source_ref, in_ref, out_ref):
    out_ref[0] = pick_rows(source_ref[...], in_ref[...])


def whole_merge(rows):
    return pl.pallas_call(
        whole_merge_kernel,
        grid=(8,),
        in_specs=[pl.BlockSpec((640, 1), lambda g: (0, 0)), pl.BlockSpec((640, 256), lambda g: (g, 0))],
        out_specs=pl.BlockSpec((1, 640, 256), lambda g: (g, 0, 0)),
        out_shape=jax.ShapeDtypeStruct((8, 640, 256), BF16),
        compiler_params=params(16),
        cost_estimate=cost(8 * 640 * 640 * 256, 5_000_000),
    )(jnp.asarray(whole_merge_source()), rows)


def forward_kernel(pieces, group, index_ref, own_ref, other_ref, own_cot_ref, other_cot_ref, *refs):
    slot_refs = refs[:pieces]
    weight_ref, dmixed_ref, acc_ref = refs[pieces : pieces + 3]
    step = pl.program_id(0)

    @pl.when(step == 0)
    def _():
        acc_ref[...] = jnp.zeros_like(acc_ref)

    if pieces == 1:
        slots = slot_refs[0][...].reshape(640, 256)
    else:
        slots_ref = refs[pieces + 3]
        for piece in range(pieces):
            slots_ref[piece * 160 : (piece + 1) * 160, :] = slot_refs[piece][...]
        slots = slots_ref[...]
    weight = pick_rows(index_ref[:, group : group + 1], slots)
    weight_ref[...] = weight
    acc_ref[:512, :] += jnp.dot(own_ref[...], weight, preferred_element_type=F32)
    acc_ref[512:, :] += jnp.dot(other_ref[...], weight, preferred_element_type=F32)

    @pl.when(step == pl.num_programs(0) - 1)
    def _():
        for half, cot_ref in enumerate((own_cot_ref, other_cot_ref)):
            rows = slice(half * 512, half * 512 + 512)
            gate = acc_ref[rows, :128]
            up = acc_ref[rows, 128:]
            cot = cot_ref[...].astype(F32)
            sig = 1.0 / (1.0 + jnp.exp(-gate))
            dmixed_ref[rows, :128] = (cot * up * sig * (1.0 + gate * (1.0 - sig))).astype(BF16)
            dmixed_ref[rows, 128:] = (cot * gate * sig).astype(BF16)


def forward(group, index, own, other, own_cot, other_cot, slots):
    pieces = len(slots)
    tokens_spec = pl.BlockSpec((512, 512), lambda b: (0, b))
    cot_spec = pl.BlockSpec((512, 128), lambda b: (0, group))
    if pieces == 1:
        slot_specs = [pl.BlockSpec((8, 80, 256), lambda b: (0, b, 0))]
    else:
        slot_specs = [pl.BlockSpec((160, 256), lambda b: (b, 0))] * pieces
    scratch = [pltpu.VMEM((1024, 256), F32)]
    if pieces > 1:
        scratch.append(pltpu.VMEM((640, 256), BF16))

    def kernel(*refs):
        forward_kernel(pieces, group, *refs)

    return pl.pallas_call(
        kernel,
        grid=(8,),
        in_specs=[pl.BlockSpec((512, 8), lambda b: (b, 0)), tokens_spec, tokens_spec, cot_spec, cot_spec] + slot_specs,
        out_specs=[pl.BlockSpec((512, 256), lambda b: (b, 0)), pl.BlockSpec((1024, 256), lambda b: (0, 0))],
        out_shape=[jax.ShapeDtypeStruct((4096, 256), BF16), jax.ShapeDtypeStruct((1024, 256), BF16)],
        scratch_shapes=scratch,
        compiler_params=params(32),
        cost_estimate=cost(1024 * 4096 * 256 + 4096 * 640 * 256, 14_000_000),
    )(index, own, other, own_cot, other_cot, *slots)


def back_kernel(refs):
    dmixed_refs, weight_refs, rest = refs[:3], refs[3:6], refs[6:]
    total = None
    for dmixed_ref, weight_ref in zip(dmixed_refs, weight_refs):
        part = lax.dot_general(
            dmixed_ref[...], weight_ref[...], (((1,), (1,)), ((), ())), preferred_element_type=F32
        )
        total = part if total is None else total + part
    if len(rest) == 2:
        total = total + rest[0][...].astype(F32)
    rest[-1][...] = total.astype(BF16)


def back(half, dmixed, weights, add=None):
    out_spec = pl.BlockSpec((512, 512), lambda b: (0, b))
    specs = [pl.BlockSpec((512, 256), lambda b: (half, 0))] * 3 + [pl.BlockSpec((512, 256), lambda b: (b, 0))] * 3
    extra = []
    if add is not None:
        specs.append(out_spec)
        extra.append(add)

    def kernel(*refs):
        back_kernel(refs)

    return pl.pallas_call(
        kernel,
        grid=(8,),
        in_specs=specs,
        out_specs=out_spec,
        out_shape=jax.ShapeDtypeStruct((512, 4096), BF16),
        compiler_params=params(32),
        cost_estimate=cost(512 * 4096 * 768, 14_000_000),
    )(*dmixed, *weights, *extra)


def moment_kernel(index_ref, in_ref, out_ref):
    out_ref[...] = pick_rows(index_ref[...], in_ref[...])


def moment_rows(index, gathered):
    count = index.shape[0]
    return pl.pallas_call(
        moment_kernel,
        grid=(6,),
        in_specs=[pl.BlockSpec((count, 1), lambda j: (0, 0)), pl.BlockSpec((1280, 256), lambda j: (0, j))],
        out_specs=pl.BlockSpec((count, 256), lambda j: (0, j)),
        out_shape=jax.ShapeDtypeStruct((count, 1536), BF16),
        compiler_params=params(32),
        cost_estimate=cost(count * 1280 * 1536, 8_000_000),
    )(index, gathered)


def assemble_kernel(place_ref, *refs):
    wide_refs, narrow_refs, out_ref, square_ref = refs[:4], refs[4:8], refs[8], refs[9]
    for ref, offset in zip(wide_refs, OFFSETS):
        rows = pl.ds(pl.multiple_of(((place_ref[0] + offset) % 4) * 128, 128), 128)
        for core in range(2):
            for group in range(2):
                for part in range(2):
                    at = core * 512 + group * 256 + part * 128
                    to = part * 768 + core * 384 + group * 128
                    out_ref[rows, to : to + 128] = ref[:, at : at + 128]
    for ref, offset in zip(narrow_refs, OFFSETS):
        chunk = ((place_ref[1] + offset) % 4) * 32
        for core in range(2):
            for part in range(2):
                at = core * 256 + part * 128
                to = part * 768 + core * 384 + 256
                for z in range(4):
                    rows = pl.ds(pl.multiple_of(z * 128 + chunk, 32), 32)
                    out_ref[rows, to : to + 128] = ref[z * 32 : (z + 1) * 32, at : at + 128]
    total = jnp.zeros((8, 128), F32)
    for step in range(16):
        rows = out_ref[step * 32 : (step + 1) * 32, :].astype(F32)
        total = total + jnp.sum((rows * rows).reshape(4, 8, 12, 128), axis=(0, 2))
    square_ref[...] = total


def assemble(place, wide, narrow):
    vmem = pl.BlockSpec(memory_space=pltpu.VMEM)
    return pl.pallas_call(
        assemble_kernel,
        in_specs=[pl.BlockSpec(memory_space=pltpu.SMEM)] + [vmem] * 8,
        out_specs=[vmem, vmem],
        out_shape=[jax.ShapeDtypeStruct((512, 1536), BF16), jax.ShapeDtypeStruct((8, 128), F32)],
        compiler_params=params(16),
        cost_estimate=cost(0, 3_200_000),
    )(place, *wide, *narrow)


def adam_kernel(square_ref, place_ref, grad_ref, moments_ref, weight_ref, new_ref, first_ref, second_ref):
    clip_norm = math.sqrt(4096 * 1536)
    factor = jnp.minimum(1.0, clip_norm / jnp.sqrt(jnp.sum(square_ref[...]) + 1e-06))
    bias_one = 1.0 - beta_one**step_count
    bias_two = 1.0 - beta_two**step_count

    def moments_next(grad, first, second):
        clipped = grad.astype(F32) * factor
        first_next = beta_one * first.astype(F32) + (1.0 - beta_one) * clipped
        second_next = beta_two * second.astype(F32) + (1.0 - beta_two) * clipped * clipped
        return first_next, second_next

    first_next, second_next = moments_next(grad_ref[...], moments_ref[:512, :], moments_ref[512:1024, :])
    update = learn_rate * (first_next / bias_one) / (jnp.sqrt(second_next / bias_two) + adam_eps)
    new_ref[...] = (weight_ref[...].astype(F32) - update).astype(BF16)
    own_grad = pick_rows(place_ref[...], grad_ref[...])
    first_own, second_own = moments_next(own_grad, moments_ref[1024:1072, :], moments_ref[1072:1120, :])
    filled = place_ref[...] >= 0
    first_ref[...] = jnp.where(filled, first_own, 0.0)
    second_ref[...] = jnp.where(filled, second_own, 0.0)


def adam(square, place, grad, moments, weight):
    wide = pl.BlockSpec((512, 256), lambda j: (0, j))
    own = pl.BlockSpec((48, 256), lambda j: (0, j))
    return pl.pallas_call(
        adam_kernel,
        grid=(6,),
        in_specs=[
            pl.BlockSpec((8, 128), lambda j: (0, 0)),
            pl.BlockSpec((48, 1), lambda j: (0, 0)),
            wide,
            pl.BlockSpec((1120, 256), lambda j: (0, j)),
            wide,
        ],
        out_specs=[wide, own, own],
        out_shape=[
            jax.ShapeDtypeStruct((512, 1536), BF16),
            jax.ShapeDtypeStruct((48, 1536), F32),
            jax.ShapeDtypeStruct((48, 1536), F32),
        ],
        compiler_params=params(32),
        cost_estimate=cost(48 * 512 * 1536, 9_000_000),
    )(square, place, grad, moments, weight)


def on_device(tokens, cotangent, old_weight, old_first, old_second, old_holder, new_owner):
    me = {axis: lax.axis_index(axis) for axis in "zxyc"}
    core = me["c"]
    dp_at = me["z"] * 4 + me["x"]
    fsdp_at = me["y"] * 2 + core

    def of_core(value, axis, other=False):
        return lax.dynamic_index_in_dim(value, 1 - core if other else core, axis, keepdims=False)

    by_half = old_weight[0].reshape(8 * SLOTS, 2, 2, 3, 128).transpose(2, 0, 3, 1, 4).reshape(2, 8 * SLOTS, 768)
    got = send(of_core(by_half, 0, other=True), "c", 1)
    chip_slots = jnp.concatenate([of_core(by_half, 0), got], axis=0)
    whole = lax.all_gather(chip_slots[:, :256], ("z", "x", "y"), axis=0, tiled=True)
    parts = gather_axis(chip_slots[:, 256:], "y")
    second, third = first_merge(parts)
    old_holder, new_owner, cotangent, tokens_late, second = lax.optimization_barrier(
        (old_holder, new_owner, cotangent, tokens, second)
    )
    second = second_merge(gather_axis(second, "x"))
    third = second_merge(gather_axis(third, "z"))
    slots = [[whole_merge(whole)], gather_axis(second, "z"), gather_axis(third, "x")]

    other_tokens = send(tokens_late, "c", 1)
    cot_half = cotangent.reshape(512, 2, 384)
    own_cot = of_core(cot_half, 1)
    other_cot = send(of_core(cot_half, 1, other=True), "c", 1)
    pair = jnp.concatenate([tokens, other_tokens], axis=0)

    holder = old_holder[:, 0].reshape(8, 512)
    order = jnp.arange(512, dtype=jnp.int32)
    before = order[None, :] < order[:, None]
    held_rank = jnp.sum(((holder[:, None, :] == holder[:, :, None]) & before[None]).astype(jnp.int32), axis=2)
    source = {"z": holder // 32, "x": holder // 8 % 4, "y": holder // 2 % 4, "c": holder % 2}
    rel = {axis: relative(source[axis], me[axis]) for axis in "zxy"}
    within = (source["c"] != core).astype(jnp.int32) * SLOTS + held_rank
    index = jnp.stack(
        [
            holder // 2 * 10 + within,
            rel["z"] * 160 + rel["x"] * 40 + rel["y"] * 10 + within,
            rel["x"] * 160 + rel["z"] * 40 + rel["y"] * 10 + within,
        ]
        + [jnp.zeros_like(within)] * 5,
        axis=-1,
    ).reshape(4096, 8)

    moments = jnp.concatenate([old_first[0].astype(BF16), old_second[0].astype(BF16)], axis=1)
    moments = moments.reshape(4, 2, 2 * SLOTS, 1536)
    chip = jnp.concatenate([of_core(moments, 1), send(of_core(moments, 1, other=True), "c", 1)], axis=1)

    def for_y(shift):
        return lax.dynamic_index_in_dim(chip, (me["y"] + shift) % 4, 0, keepdims=False)

    shard_moments = jnp.concatenate([for_y(0)] + [send(for_y(shift), "y", shift) for shift in SHIFTS], axis=0)
    all_moments = lax.all_gather(shard_moments, ("z", "x"), axis=0, tiled=True)

    weights, dmixed, grads = [None] * 3, [None] * 3, [None] * 3
    for group in (1, 2, 0):
        weights[group], dmixed[group] = forward(group, index, tokens, other_tokens, own_cot, other_cot, slots[group])
        grads[group] = lax.dot_general(
            pair, dmixed[group], (((0,), (0,)), ((), ())), preferred_element_type=F32
        ).astype(BF16)

    late = lax.optimization_barrier((*dmixed, *weights, *grads))
    dmixed, weights, grads = late[:3], late[3:6], late[6:]

    partner_part = send(back(1, dmixed, weights), "c", 1)
    input_grad = back(0, dmixed, weights, partner_part)

    shard_weights = jnp.stack(
        [lax.dynamic_slice_in_dim(weight, me["y"] * 1024, 1024, 0).reshape(2, 512, 2, 128) for weight in weights], axis=3
    )
    keep = of_core(shard_weights, 0)
    recv = send(of_core(shard_weights, 0, other=True), "c", 1)
    low = jnp.where(core == 0, keep, recv)
    high = jnp.where(core == 0, recv, keep)
    shard_w = jnp.stack([low, high], axis=2).reshape(512, 1536)

    my_holder = lax.dynamic_index_in_dim(holder, fsdp_at, 0, keepdims=False)
    my_rank = lax.dynamic_index_in_dim(held_rank, fsdp_at, 0, keepdims=False)
    moment_at = (
        my_holder // 8 * 80
        + relative(my_holder // 2 % 4, me["y"]) * 20
        + (my_holder % 2 != core).astype(jnp.int32) * 10
        + my_rank
    )
    owner = lax.dynamic_index_in_dim(new_owner[:, 0].reshape(8, 512), fsdp_at, 0, keepdims=False)
    own_rank = jnp.sum(((owner[None, :] == owner[:, None]) & before).astype(jnp.int32), axis=1)
    picked = (owner == dp_at)[None, :] & (own_rank[None, :] == jnp.arange(48, dtype=jnp.int32)[:, None])
    own_place = jnp.sum(jnp.where(picked, order[None, :] + 1, 0), axis=1) - 1
    own_moment_at = jnp.sum(jnp.where(picked, moment_at[None, :] + 1, 0), axis=1) - 1
    own_second_at = jnp.where(own_moment_at >= 0, own_moment_at + SLOTS, -1)
    moment_index = jnp.concatenate([moment_at, moment_at + SLOTS, own_moment_at, own_second_at])[:, None]
    moment_values = moment_rows(moment_index, all_moments)

    def scatter(value, dim, axis):
        def chunk(shift):
            return lax.dynamic_index_in_dim(value, (me[axis] + shift) % 4, dim, keepdims=False)

        parts = [chunk(0)] + [send(chunk(shift), axis, shift) for shift in SHIFTS]
        return symmetric_sum(parts).astype(BF16)

    values = [grad.reshape(4, 2, 4, 4, 32, 256) for grad in grads]
    values = [scatter(values[0], 0, "y"), scatter(values[1], 2, "z"), scatter(values[2], 3, "x")]
    values = [scatter(values[0], 1, "z"), scatter(values[1], 0, "y"), scatter(values[2], 0, "y")]
    values = [value.reshape(2, 128, 256) for value in values]

    def both_cores(value):
        keep = of_core(value, 0)
        recv = send(of_core(value, 0, other=True), "c", 1)
        return jnp.concatenate([jnp.where(core == 0, keep, recv), jnp.where(core == 0, recv, keep)], axis=-1)

    wide = both_cores(jnp.concatenate(values[:2], axis=-1))
    narrow = both_cores(values[2])
    wide = symmetric_sum(gather_axis(wide, "x")).astype(BF16)
    narrow = symmetric_sum(gather_axis(narrow, "z")).astype(BF16)
    wide, narrow, input_grad, shard_w, moment_values = lax.optimization_barrier(
        (wide, narrow, input_grad, shard_w, moment_values)
    )
    place = jnp.stack([me["z"], me["x"]]).astype(jnp.int32)
    summed, square = assemble(place, gather_axis(wide, "z"), gather_axis(narrow, "x"))
    square = square + send(square, "c", 1)
    square = symmetric_sum(gather_axis(square, "y"))
    new_shard, first_out, second_out = adam(square, own_place[:, None], summed, moment_values, shard_w)
    return (input_grad, new_shard, first_out[None, None], second_out[None, None])


def solution(mesh):
    chips = Mesh(mesh.devices.reshape(4, 4, 4, 2), ("z", "x", "y", "c"))
    every = ("z", "x", "y", "c")
    placed = (
        P(every, None),
        P(every, None),
        P(every, None, None, None),
        P(every, None, None, None),
        P(every, None, None, None),
        P(),
        P(),
    )
    return jax.shard_map(
        on_device,
        mesh=chips,
        in_specs=placed,
        out_specs=(
            P(every, None),
            P(("y", "c"), None),
            P(("y", "c"), ("z", "x"), None, None),
            P(("y", "c"), ("z", "x"), None, None),
        ),
        check_vma=False,
    )
```

```python
import math

import jax
import jax.numpy as jnp
import numpy as np
from jax import lax
from jax.experimental import pallas as pl
from jax.experimental.pallas import tpu as pltpu
from jax.sharding import Mesh
from jax.sharding import PartitionSpec as P

beta_one = 0.9
beta_two = 0.999
learn_rate = 0.01
adam_eps = 1e-08
step_count = 100

SIZE = {"z": 4, "x": 4, "y": 4, "c": 2}
SHIFTS = (1, 3, 2)
OFFSETS = (0, 3, 1, 2)
SLOTS = 5
BF16 = jnp.bfloat16
F32 = jnp.float32


def send(value, axis, shift):
    size = SIZE[axis]
    return lax.ppermute(value, axis, [(i, (i + shift) % size) for i in range(size)])


def gather_axis(block, axis):
    return [block] + [send(block, axis, shift) for shift in SHIFTS]


def relative(source, mine):
    away = (source - mine) % 4
    return jnp.where(away == 0, 0, jnp.where(away == 3, 1, jnp.where(away == 1, 2, 3)))


def symmetric_sum(parts):
    own, left, right, across = [part.astype(F32) for part in parts]
    return (own + across) + (left + right)


def pick_rows(index, rows):
    lanes = lax.broadcasted_iota(jnp.int32, (index.shape[0], rows.shape[0]), 1)
    pick = (index == lanes).astype(BF16)
    return jnp.dot(pick, rows, preferred_element_type=F32).astype(BF16)


def params(mib):
    return pltpu.CompilerParams(vmem_limit_bytes=mib * 1024 * 1024)


def cost(macs, moved):
    return pl.CostEstimate(flops=2 * macs, bytes_accessed=moved, transcendentals=0)


def whole_merge_source():
    i = np.arange(640)
    b, chip, core, k = i // 80, i // 10 % 8, i // 5 % 2, i % 5
    return (chip * 80 + core * 40 + b * 5 + k).astype(np.int32)[:, None]


def forward_kernel(
    source_ref, index_ref, slots_ref, own_ref, other_ref, own_cot_ref, other_cot_ref, weight_ref, dmixed_ref, acc_ref, placed_ref
):
    step = pl.program_id(0)

    @pl.when(step == 0)
    def _():
        acc_ref[...] = jnp.zeros_like(acc_ref)

    @pl.when(step < 8)
    def _():
        placed = pick_rows(source_ref[...], slots_ref[...])
        for b in range(8):
            placed_ref[b, pl.ds(pl.multiple_of(step * 80, 16), 80), :] = placed[b * 80 : (b + 1) * 80, :]

    @pl.when(step >= 8)
    def _():
        weight = pick_rows(index_ref[...], placed_ref[step - 8])
        weight_ref[...] = weight
        acc_ref[:512, :] += jnp.dot(own_ref[...], weight, preferred_element_type=F32)
        acc_ref[512:, :] += jnp.dot(other_ref[...], weight, preferred_element_type=F32)

    @pl.when(step == 15)
    def _():
        for half, cot_ref in enumerate((own_cot_ref, other_cot_ref)):
            rows = slice(half * 512, half * 512 + 512)
            for group in range(3):
                at = group * 256
                gate = acc_ref[rows, at : at + 128]
                up = acc_ref[rows, at + 128 : at + 256]
                cot = cot_ref[:, group * 128 : (group + 1) * 128].astype(F32)
                sig = 1.0 / (1.0 + jnp.exp(-gate))
                dmixed_ref[rows, at : at + 128] = (cot * up * sig * (1.0 + gate * (1.0 - sig))).astype(BF16)
                dmixed_ref[rows, at + 128 : at + 256] = (cot * gate * sig).astype(BF16)


def forward(index, slots, own, other, own_cot, other_cot):
    def later(step):
        return jnp.maximum(step - 8, 0)

    tokens_spec = pl.BlockSpec((512, 512), lambda i: (0, later(i)))
    cot_spec = pl.BlockSpec((512, 384), lambda i: (0, 0))
    return pl.pallas_call(
        forward_kernel,
        grid=(16,),
        in_specs=[
            pl.BlockSpec((640, 1), lambda i: (0, 0)),
            pl.BlockSpec((512, 1), lambda i: (later(i), 0)),
            pl.BlockSpec((640, 768), lambda i: (jnp.minimum(i, 7), 0)),
            tokens_spec,
            tokens_spec,
            cot_spec,
            cot_spec,
        ],
        out_specs=[pl.BlockSpec((512, 768), lambda i: (later(i), 0)), pl.BlockSpec((1024, 768), lambda i: (0, 0))],
        out_shape=[jax.ShapeDtypeStruct((4096, 768), BF16), jax.ShapeDtypeStruct((1024, 768), BF16)],
        scratch_shapes=[pltpu.VMEM((1024, 768), F32), pltpu.VMEM((8, 640, 768), BF16)],
        compiler_params=params(48),
        cost_estimate=cost(1024 * 4096 * 768 + 4096 * 640 * 768 + 8 * 640 * 640 * 768, 24_000_000),
    )(jnp.asarray(whole_merge_source()), index, slots, own, other, own_cot, other_cot)


def back_kernel(dmixed_ref, weight_ref, *rest):
    total = lax.dot_general(dmixed_ref[...], weight_ref[...], (((1,), (1,)), ((), ())), preferred_element_type=F32)
    if len(rest) == 2:
        total = total + rest[0][...].astype(F32)
    rest[-1][...] = total.astype(BF16)


def back(half, dmixed, weight, add=None):
    out_spec = pl.BlockSpec((512, 512), lambda b: (0, b))
    specs = [pl.BlockSpec((512, 768), lambda b: (half, 0)), pl.BlockSpec((512, 768), lambda b: (b, 0))]
    extra = []
    if add is not None:
        specs.append(out_spec)
        extra.append(add)
    return pl.pallas_call(
        back_kernel,
        grid=(8,),
        in_specs=specs,
        out_specs=out_spec,
        out_shape=jax.ShapeDtypeStruct((512, 4096), BF16),
        compiler_params=params(32),
        cost_estimate=cost(512 * 4096 * 768, 14_000_000),
    )(dmixed, weight, *extra)


def moment_kernel(index_ref, *refs):
    pieces, out_ref, rows_ref = refs[:4], refs[4], refs[5]
    for piece in range(4):
        rows_ref[piece * 320 : (piece + 1) * 320, :] = pieces[piece][...]
    out_ref[...] = pick_rows(index_ref[...], rows_ref[...])


def moment_rows(index, pieces):
    count = index.shape[0]
    return pl.pallas_call(
        moment_kernel,
        grid=(3,),
        in_specs=[pl.BlockSpec((count, 1), lambda j: (0, 0))] + [pl.BlockSpec((320, 256), lambda j: (0, j))] * 4,
        out_specs=pl.BlockSpec((count, 256), lambda j: (0, j)),
        out_shape=jax.ShapeDtypeStruct((count, 768), BF16),
        scratch_shapes=[pltpu.VMEM((1280, 256), BF16)],
        compiler_params=params(32),
        cost_estimate=cost(count * 1280 * 768, 4_000_000),
    )(index, *pieces)


def assemble_kernel(place_ref, *refs):
    wide_refs, narrow_refs, out_ref, square_ref = refs[:4], refs[4:8], refs[8], refs[9]
    for ref, offset in zip(wide_refs, OFFSETS):
        rows = pl.ds(pl.multiple_of(((place_ref[0] + offset) % 4) * 128, 128), 128)
        for core in range(2):
            for group in range(2):
                for part in range(2):
                    at = core * 512 + group * 256 + part * 128
                    to = part * 768 + core * 384 + group * 128
                    out_ref[rows, to : to + 128] = ref[:, at : at + 128]
    for ref, offset in zip(narrow_refs, OFFSETS):
        chunk = ((place_ref[1] + offset) % 4) * 32
        for core in range(2):
            for part in range(2):
                at = core * 256 + part * 128
                to = part * 768 + core * 384 + 256
                for z in range(4):
                    rows = pl.ds(pl.multiple_of(z * 128 + chunk, 32), 32)
                    out_ref[rows, to : to + 128] = ref[z * 32 : (z + 1) * 32, at : at + 128]
    total = jnp.zeros((8, 128), F32)
    for step in range(16):
        rows = out_ref[step * 32 : (step + 1) * 32, :].astype(F32)
        total = total + jnp.sum((rows * rows).reshape(4, 8, 12, 128), axis=(0, 2))
    square_ref[...] = total


def assemble(place, wide, narrow):
    vmem = pl.BlockSpec(memory_space=pltpu.VMEM)
    return pl.pallas_call(
        assemble_kernel,
        in_specs=[pl.BlockSpec(memory_space=pltpu.SMEM)] + [vmem] * 8,
        out_specs=[vmem, vmem],
        out_shape=[jax.ShapeDtypeStruct((512, 1536), BF16), jax.ShapeDtypeStruct((8, 128), F32)],
        compiler_params=params(16),
        cost_estimate=cost(0, 3_200_000),
    )(place, *wide, *narrow)


def adam_kernel(core_ref, square_ref, place_ref, grad_ref, moments_ref, *refs):
    keep_refs, recv_refs, (new_ref, first_ref, second_ref) = refs[:3], refs[3:6], refs[6:]
    clip_norm = math.sqrt(4096 * 1536)
    factor = jnp.minimum(1.0, clip_norm / jnp.sqrt(jnp.sum(square_ref[...]) + 1e-06))
    bias_one = 1.0 - beta_one**step_count
    bias_two = 1.0 - beta_two**step_count
    kept = pl.program_id(0) % 2 == core_ref[0]

    def moments_next(grad, first, second):
        clipped = grad.astype(F32) * factor
        first_next = beta_one * first.astype(F32) + (1.0 - beta_one) * clipped
        second_next = beta_two * second.astype(F32) + (1.0 - beta_two) * clipped * clipped
        return first_next, second_next

    for group in range(3):
        at = slice(group * 128, (group + 1) * 128)
        first_next, second_next = moments_next(grad_ref[:, at], moments_ref[:512, at], moments_ref[512:1024, at])
        update = first_next * (learn_rate / bias_one) / (jnp.sqrt(second_next * (1.0 / bias_two)) + adam_eps)
        weight = jnp.where(kept, keep_refs[group][...].astype(F32), recv_refs[group][...].astype(F32))
        new_ref[:, at] = (weight - update).astype(BF16)
    own_grad = pick_rows(place_ref[...], grad_ref[...])
    first_own, second_own = moments_next(own_grad, moments_ref[1024:1072, :], moments_ref[1072:1120, :])
    filled = place_ref[...] >= 0
    first_ref[...] = jnp.where(filled, first_own, 0.0)
    second_ref[...] = jnp.where(filled, second_own, 0.0)


def adam(core, square, place, grad, moments, keep, recv):
    wide = pl.BlockSpec((512, 384), lambda j: (0, j))
    own = pl.BlockSpec((48, 384), lambda j: (0, j))
    weight_specs = [pl.BlockSpec((512, 128), lambda j, group=group: (0, group * 2 + j // 2)) for group in range(3)]
    return pl.pallas_call(
        adam_kernel,
        grid=(4,),
        in_specs=[
            pl.BlockSpec(memory_space=pltpu.SMEM),
            pl.BlockSpec((8, 128), lambda j: (0, 0)),
            pl.BlockSpec((48, 1), lambda j: (0, 0)),
            wide,
            pl.BlockSpec((1120, 384), lambda j: (0, j)),
        ]
        + weight_specs * 2,
        out_specs=[wide, own, own],
        out_shape=[
            jax.ShapeDtypeStruct((512, 1536), BF16),
            jax.ShapeDtypeStruct((48, 1536), F32),
            jax.ShapeDtypeStruct((48, 1536), F32),
        ],
        compiler_params=params(32),
        cost_estimate=cost(48 * 512 * 1536, 9_000_000),
    )(core, square, place, grad, moments, keep, keep, keep, recv, recv, recv)


def on_device(tokens, cotangent, old_weight, old_first, old_second, old_holder, new_owner):
    me = {axis: lax.axis_index(axis) for axis in "zxyc"}
    core = me["c"]
    dp_at = me["z"] * 4 + me["x"]
    fsdp_at = me["y"] * 2 + core

    def of_core(value, axis, other=False):
        return lax.dynamic_index_in_dim(value, 1 - core if other else core, axis, keepdims=False)

    by_half = old_weight[0].reshape(8 * SLOTS, 2, 2, 3, 128).transpose(2, 0, 3, 1, 4).reshape(2, 8 * SLOTS, 768)
    got = send(of_core(by_half, 0, other=True), "c", 1)
    chip_slots = jnp.concatenate([of_core(by_half, 0), got], axis=0)
    chip_slots, tokens, cotangent, old_first, old_second, old_holder, new_owner = lax.optimization_barrier(
        (chip_slots, tokens, cotangent, old_first, old_second, old_holder, new_owner)
    )
    slots = lax.all_gather(chip_slots, ("z", "x", "y"), axis=0, tiled=True)

    moments = jnp.concatenate([old_first[0].astype(BF16), old_second[0].astype(BF16)], axis=1)
    moments = moments.reshape(4, 2, 2 * SLOTS, 1536)
    chip = jnp.concatenate([of_core(moments, 1), send(of_core(moments, 1, other=True), "c", 1)], axis=1)

    def for_y(shift):
        return lax.dynamic_index_in_dim(chip, (me["y"] + shift) % 4, 0, keepdims=False)

    shard_moments = jnp.concatenate([for_y(0)] + [send(for_y(shift), "y", shift) for shift in SHIFTS], axis=0)
    halves = [
        jnp.concatenate(gather_axis(shard_moments[:, :768], "z"), axis=0),
        jnp.concatenate(gather_axis(shard_moments[:, 768:], "x"), axis=0),
    ]
    halves = [gather_axis(halves[0], "x"), gather_axis(halves[1], "z")]

    other_tokens = send(tokens, "c", 1)
    cot_half = cotangent.reshape(512, 2, 384)
    own_cot = of_core(cot_half, 1)
    other_cot = send(of_core(cot_half, 1, other=True), "c", 1)
    pair = jnp.concatenate([tokens, other_tokens], axis=0)

    holder = old_holder[:, 0].reshape(8, 512)
    order = jnp.arange(512, dtype=jnp.int32)
    before = order[None, :] < order[:, None]
    held_rank = jnp.sum(((holder[:, None, :] == holder[:, :, None]) & before[None]).astype(jnp.int32), axis=2)
    index = (holder // 2 * 10 + (holder % 2 != core).astype(jnp.int32) * SLOTS + held_rank).reshape(4096, 1)

    my_holder = lax.dynamic_index_in_dim(holder, fsdp_at, 0, keepdims=False)
    my_rank = lax.dynamic_index_in_dim(held_rank, fsdp_at, 0, keepdims=False)
    within = (
        relative(my_holder // 2 % 4, me["y"]) * 20 + (my_holder % 2 != core).astype(jnp.int32) * 10 + my_rank
    )
    rel_z = relative(my_holder // 32, me["z"])
    rel_x = relative(my_holder // 8 % 4, me["x"])
    owner = lax.dynamic_index_in_dim(new_owner[:, 0].reshape(8, 512), fsdp_at, 0, keepdims=False)
    own_rank = jnp.sum(((owner[None, :] == owner[:, None]) & before).astype(jnp.int32), axis=1)
    picked = (owner == dp_at)[None, :] & (own_rank[None, :] == jnp.arange(48, dtype=jnp.int32)[:, None])
    own_place = jnp.sum(jnp.where(picked, order[None, :] + 1, 0), axis=1) - 1

    def moment_index(at):
        own_at = jnp.sum(jnp.where(picked, at[None, :] + 1, 0), axis=1) - 1
        own_second_at = jnp.where(own_at >= 0, own_at + SLOTS, -1)
        return jnp.concatenate([at, at + SLOTS, own_at, own_second_at])[:, None]

    moment_values = jnp.concatenate(
        [
            moment_rows(moment_index(rel_x * 320 + rel_z * 80 + within), halves[0]),
            moment_rows(moment_index(rel_z * 320 + rel_x * 80 + within), halves[1]),
        ],
        axis=1,
    )
    slots, index, other_tokens, own_cot, other_cot, pair, moment_values, own_place = lax.optimization_barrier(
        (slots, index, other_tokens, own_cot, other_cot, pair, moment_values, own_place)
    )

    weight, dmixed = forward(index, slots, tokens, other_tokens, own_cot, other_cot)
    grads = [
        lax.dot_general(
            pair, dmixed[:, group * 256 : (group + 1) * 256], (((0,), (0,)), ((), ())), preferred_element_type=F32
        ).astype(BF16)
        for group in range(3)
    ]
    grads[1], grads[2], dmixed, weight = lax.optimization_barrier((grads[1], grads[2], dmixed, weight))

    def scatter(value, dim, axis):
        def chunk(shift):
            return lax.dynamic_index_in_dim(value, (me[axis] + shift) % 4, dim, keepdims=False)

        parts = [chunk(0)] + [send(chunk(shift), axis, shift) for shift in SHIFTS]
        return symmetric_sum(parts).astype(BF16)

    by_y = lax.psum_scatter(grads[0], "y", scatter_dimension=0, tiled=True).reshape(2, 4, 4, 32, 256)
    by_z = scatter(grads[1].reshape(4, 2, 4, 4, 32, 256), 2, "z").reshape(4, 2, 128, 256)
    by_x = scatter(grads[2].reshape(4, 2, 4, 4, 32, 256), 3, "x").reshape(4, 2, 128, 256)

    other_part = back(1, dmixed, weight)
    shard_weight = lax.dynamic_slice_in_dim(weight, me["y"] * 1024, 1024, 0).reshape(2, 512, 768)
    weight_keep = of_core(shard_weight, 0)
    weight_give = of_core(shard_weight, 0, other=True)
    by_z, by_x, other_part, weight_give = lax.optimization_barrier((by_z, by_x, other_part, weight_give))
    partner_part = send(other_part, "c", 1)
    weight_recv = send(weight_give, "c", 1)

    rest = scatter(jnp.concatenate([by_z, by_x], axis=-1), 0, "y")
    by_y = scatter(by_y, 1, "z").reshape(2, 128, 256)
    value = jnp.concatenate([by_y, rest], axis=-1)
    give = of_core(value, 0, other=True)
    keep, give, partner_part, weight_recv = lax.optimization_barrier(
        (of_core(value, 0), give, partner_part, weight_recv)
    )
    input_grad = back(0, dmixed, weight, partner_part)
    recv = send(give, "c", 1)
    low = jnp.where(core == 0, keep, recv)
    high = jnp.where(core == 0, recv, keep)
    wide = jnp.concatenate([low[:, :512], high[:, :512]], axis=1)
    narrow = jnp.concatenate([low[:, 512:], high[:, 512:]], axis=1)
    wide = symmetric_sum(gather_axis(wide, "x")).astype(BF16)
    narrow = symmetric_sum(gather_axis(narrow, "z")).astype(BF16)
    wide, narrow, input_grad = lax.optimization_barrier((wide, narrow, input_grad))
    place = jnp.stack([me["z"], me["x"]]).astype(jnp.int32)
    summed, square = assemble(place, gather_axis(wide, "z"), gather_axis(narrow, "x"))
    square = square + send(square, "c", 1)
    square = symmetric_sum(gather_axis(square, "y"))
    new_shard, first_out, second_out = adam(
        core.astype(jnp.int32)[None], square, own_place[:, None], summed, moment_values, weight_keep, weight_recv
    )
    return (input_grad, new_shard, first_out[None, None], second_out[None, None])


def solution(mesh):
    chips = Mesh(mesh.devices.reshape(4, 4, 4, 2), ("z", "x", "y", "c"))
    every = ("z", "x", "y", "c")
    placed = (
        P(every, None),
        P(every, None),
        P(every, None, None, None),
        P(every, None, None, None),
        P(every, None, None, None),
        P(),
        P(),
    )
    return jax.shard_map(
        on_device,
        mesh=chips,
        in_specs=placed,
        out_specs=(
            P(every, None),
            P(("y", "c"), None),
            P(("y", "c"), ("z", "x"), None, None),
            P(("y", "c"), ("z", "x"), None, None),
        ),
        check_vma=False,
    )
```

```python
import math

import jax
import jax.numpy as jnp
import numpy as np
from jax import lax
from jax.experimental import pallas as pl
from jax.experimental.pallas import tpu as pltpu
from jax.sharding import Mesh
from jax.sharding import PartitionSpec as P

beta_one = 0.9
beta_two = 0.999
learn_rate = 0.01
adam_eps = 1e-08
step_count = 100

SIZE = {"z": 4, "x": 4, "y": 4, "c": 2}
SHIFTS = (1, 3, 2)
OFFSETS = (0, 3, 1, 2)
SLOTS = 5
BF16 = jnp.bfloat16
F32 = jnp.float32


def send(value, axis, shift):
    size = SIZE[axis]
    return lax.ppermute(value, axis, [(i, (i + shift) % size) for i in range(size)])


def send_by_core(value, axis, shift):
    pairs = [(i * 2 + c, (i + (shift if c == 0 else 4 - shift)) % 4 * 2 + c) for i in range(4) for c in range(2)]
    return lax.ppermute(value, (axis, "c"), pairs)


def gather_axis(block, axis):
    return [block] + [send(block, axis, shift) for shift in SHIFTS]


def relative(source, mine):
    away = (source - mine) % 4
    return jnp.where(away == 0, 0, jnp.where(away == 3, 1, jnp.where(away == 1, 2, 3)))


def symmetric_sum(parts):
    own, left, right, across = [part.astype(F32) for part in parts]
    return (own + across) + (left + right)


def pick_rows(index, rows):
    lanes = lax.broadcasted_iota(jnp.int32, (index.shape[0], rows.shape[0]), 1)
    pick = (index == lanes).astype(BF16)
    return jnp.dot(pick, rows, preferred_element_type=F32).astype(BF16)


def params(mib):
    return pltpu.CompilerParams(vmem_limit_bytes=mib * 1024 * 1024)


def cost(macs, moved):
    return pl.CostEstimate(flops=2 * macs, bytes_accessed=moved, transcendentals=0)


def chip_merge_source():
    i = np.arange(320)
    b, chip, core, k = i // 40, i // 10 % 4, i // 5 % 2, i % 5
    return (chip * 80 + core * 40 + b * 5 + k).astype(np.int32)[:, None]


def chip_merge_kernel(source_ref, a_ref, b_ref, c_ref, d_ref, out_ref, rows_ref):
    for piece, ref in enumerate((a_ref, b_ref, c_ref, d_ref)):
        rows_ref[piece * 80 : (piece + 1) * 80, :] = ref[...]
    out_ref[...] = pick_rows(source_ref[...], rows_ref[...])


def chip_merge(parts):
    return pl.pallas_call(
        chip_merge_kernel,
        out_shape=jax.ShapeDtypeStruct((320, 768), BF16),
        scratch_shapes=[pltpu.VMEM((320, 768), BF16)],
        compiler_params=params(16),
        cost_estimate=cost(320 * 320 * 768, 1_000_000),
    )(jnp.asarray(chip_merge_source()), *parts)


def forward_kernel(
    index_ref, slots_ref, own_ref, other_ref, own_cot_ref, other_cot_ref, weight_ref, dmixed_ref, acc_ref, rows_ref
):
    step = pl.program_id(0)

    @pl.when(step == 0)
    def _():
        acc_ref[...] = jnp.zeros_like(acc_ref)

    for b in range(2):
        for chip in range(16):
            rows_ref[b, chip * 40 : (chip + 1) * 40, :] = slots_ref[chip, b * 40 : (b + 1) * 40, :]
        weight_ref[b * 512 : (b + 1) * 512, :] = pick_rows(index_ref[b * 512 : (b + 1) * 512, :], rows_ref[b])
    acc_ref[:512, :] += jnp.dot(own_ref[...], weight_ref[...], preferred_element_type=F32)
    acc_ref[512:, :] += jnp.dot(other_ref[...], weight_ref[...], preferred_element_type=F32)

    @pl.when(step == 3)
    def _():
        for half, cot_ref in enumerate((own_cot_ref, other_cot_ref)):
            rows = slice(half * 512, half * 512 + 512)
            for group in range(3):
                gate = acc_ref[rows, group * 256 : group * 256 + 128]
                up = acc_ref[rows, group * 256 + 128 : group * 256 + 256]
                cot = cot_ref[:, group * 128 : (group + 1) * 128].astype(F32)
                sig = 1.0 / (1.0 + jnp.exp(-gate))
                at = group * 256
                dmixed_ref[rows, at : at + 128] = (cot * up * sig * (1.0 + gate * (1.0 - sig))).astype(BF16)
                dmixed_ref[rows, at + 128 : at + 256] = (cot * gate * sig).astype(BF16)


def forward(index, slots, own, other, own_cot, other_cot):
    tokens_spec = pl.BlockSpec((512, 1024), lambda i: (0, i))
    cot_spec = pl.BlockSpec((512, 384), lambda i: (0, 0))
    return pl.pallas_call(
        forward_kernel,
        grid=(4,),
        in_specs=[
            pl.BlockSpec((1024, 1), lambda i: (i, 0)),
            pl.BlockSpec((16, 80, 768), lambda i: (0, i, 0)),
            tokens_spec,
            tokens_spec,
            cot_spec,
            cot_spec,
        ],
        out_specs=[pl.BlockSpec((1024, 768), lambda i: (i, 0)), pl.BlockSpec((1024, 768), lambda i: (0, 0))],
        out_shape=[jax.ShapeDtypeStruct((4096, 768), BF16), jax.ShapeDtypeStruct((1024, 768), BF16)],
        scratch_shapes=[pltpu.VMEM((1024, 768), F32), pltpu.VMEM((2, 640, 768), BF16)],
        compiler_params=params(36),
        cost_estimate=cost(1024 * 4096 * 768 + 4096 * 640 * 768, 24_000_000),
    )(index, slots.reshape(16, 320, 768), own, other, own_cot, other_cot)


def back_kernel(dmixed_ref, weight_ref, *rest):
    total = lax.dot_general(dmixed_ref[...], weight_ref[...], (((1,), (1,)), ((), ())), preferred_element_type=F32)
    if len(rest) == 2:
        total = total + rest[0][...].astype(F32)
    rest[-1][...] = total.astype(BF16)


def back(half, dmixed, weight, add=None):
    out_spec = pl.BlockSpec((512, 512), lambda b: (0, b))
    specs = [pl.BlockSpec((512, 768), lambda b: (half, 0)), pl.BlockSpec((512, 768), lambda b: (b, 0))]
    extra = []
    if add is not None:
        specs.append(out_spec)
        extra.append(add)
    return pl.pallas_call(
        back_kernel,
        grid=(8,),
        in_specs=specs,
        out_specs=out_spec,
        out_shape=jax.ShapeDtypeStruct((512, 4096), BF16),
        compiler_params=params(32),
        cost_estimate=cost(512 * 4096 * 768, 14_000_000),
    )(dmixed, weight, *extra)


def moment_kernel(index_ref, in_ref, out_ref):
    out_ref[...] = pick_rows(index_ref[...], in_ref[...])


def moment_rows(index, gathered):
    count = index.shape[0]
    return pl.pallas_call(
        moment_kernel,
        grid=(3,),
        in_specs=[pl.BlockSpec((count, 1), lambda j: (0, 0)), pl.BlockSpec((1280, 512), lambda j: (0, j))],
        out_specs=pl.BlockSpec((count, 512), lambda j: (0, j)),
        out_shape=jax.ShapeDtypeStruct((count, 1536), BF16),
        compiler_params=params(56),
        cost_estimate=cost(count * 1280 * 1536, 8_000_000),
    )(index, gathered)


def assemble_kernel(place_ref, *refs):
    out_ref, square_ref = refs[8], refs[9]
    for which, groups in enumerate(((0, 1), (2,))):
        for ref, offset in zip(refs[which * 4 : which * 4 + 4], OFFSETS):
            rows = pl.ds(pl.multiple_of(((place_ref[which] + offset) % 4) * 128, 128), 128)
            for core in range(2):
                for nth, group in enumerate(groups):
                    for part in range(2):
                        at = core * 256 * len(groups) + nth * 256 + part * 128
                        to = part * 768 + core * 384 + group * 128
                        out_ref[rows, to : to + 128] = ref[:, at : at + 128]
    total = jnp.zeros((8, 128), F32)
    for step in range(16):
        rows = out_ref[step * 32 : (step + 1) * 32, :].astype(F32)
        total = total + jnp.sum((rows * rows).reshape(4, 8, 12, 128), axis=(0, 2))
    square_ref[...] = total


def assemble(place, left, right):
    vmem = pl.BlockSpec(memory_space=pltpu.VMEM)
    return pl.pallas_call(
        assemble_kernel,
        in_specs=[pl.BlockSpec(memory_space=pltpu.SMEM)] + [vmem] * 8,
        out_specs=[vmem, vmem],
        out_shape=[jax.ShapeDtypeStruct((512, 1536), BF16), jax.ShapeDtypeStruct((8, 128), F32)],
        compiler_params=params(16),
        cost_estimate=cost(0, 3_200_000),
    )(place, *left, *right)


def adam_kernel(core_ref, square_ref, place_ref, grad_ref, moments_ref, *refs):
    keep_refs, recv_refs, (new_ref, first_ref, second_ref) = refs[:3], refs[3:6], refs[6:]
    clip_norm = math.sqrt(4096 * 1536)
    factor = jnp.minimum(1.0, clip_norm / jnp.sqrt(jnp.sum(square_ref[...]) + 1e-06))
    bias_one = 1.0 - beta_one**step_count
    bias_two = 1.0 - beta_two**step_count
    kept = pl.program_id(0) % 2 == core_ref[0]

    def moments_next(grad, first, second):
        clipped = grad.astype(F32) * factor
        first_next = beta_one * first.astype(F32) + (1.0 - beta_one) * clipped
        second_next = beta_two * second.astype(F32) + (1.0 - beta_two) * clipped * clipped
        return first_next, second_next

    for group in range(3):
        at = slice(group * 128, (group + 1) * 128)
        first_next, second_next = moments_next(grad_ref[:, at], moments_ref[:512, at], moments_ref[512:1024, at])
        scaled = second_next * (1.0 / bias_two)
        update = first_next * (learn_rate / bias_one) / (scaled * lax.rsqrt(scaled) + adam_eps)
        weight = jnp.where(kept, keep_refs[group][...].astype(F32), recv_refs[group][...].astype(F32))
        new_ref[:, at] = (weight - update).astype(BF16)
    own_grad = pick_rows(place_ref[...], grad_ref[...])
    first_own, second_own = moments_next(own_grad, moments_ref[1024:1072, :], moments_ref[1072:1120, :])
    filled = place_ref[...] >= 0
    first_ref[...] = jnp.where(filled, first_own, 0.0)
    second_ref[...] = jnp.where(filled, second_own, 0.0)


def adam(core, square, place, grad, moments, keep, recv):
    wide = pl.BlockSpec((512, 384), lambda j: (0, j))
    own = pl.BlockSpec((48, 384), lambda j: (0, j))
    weight_specs = [pl.BlockSpec((512, 128), lambda j, group=group: (0, group * 2 + j // 2)) for group in range(3)]
    return pl.pallas_call(
        adam_kernel,
        grid=(4,),
        in_specs=[
            pl.BlockSpec(memory_space=pltpu.SMEM),
            pl.BlockSpec((8, 128), lambda j: (0, 0)),
            pl.BlockSpec((48, 1), lambda j: (0, 0)),
            wide,
            pl.BlockSpec((1120, 384), lambda j: (0, j)),
        ]
        + weight_specs * 2,
        out_specs=[wide, own, own],
        out_shape=[
            jax.ShapeDtypeStruct((512, 1536), BF16),
            jax.ShapeDtypeStruct((48, 1536), F32),
            jax.ShapeDtypeStruct((48, 1536), F32),
        ],
        compiler_params=params(56),
        cost_estimate=cost(48 * 512 * 1536, 9_000_000),
    )(core, square, place, grad, moments, keep, keep, keep, recv, recv, recv)


def on_device(tokens, cotangent, old_weight, old_first, old_second, old_holder, new_owner):
    me = {axis: lax.axis_index(axis) for axis in "zxyc"}
    core = me["c"]
    dp_at = me["z"] * 4 + me["x"]
    fsdp_at = me["y"] * 2 + core

    def of_core(value, axis, other=False):
        return lax.dynamic_index_in_dim(value, 1 - core if other else core, axis, keepdims=False)

    by_half = old_weight[0].reshape(8 * SLOTS, 2, 2, 3, 128).transpose(2, 0, 3, 1, 4).reshape(2, 8 * SLOTS, 768)
    got = send(of_core(by_half, 0, other=True), "c", 1)
    chip_slots = jnp.concatenate([of_core(by_half, 0), got], axis=0)
    chip_slots = chip_merge(gather_axis(chip_slots, "y"))
    tokens, cotangent, old_first, old_second, old_holder, new_owner, chip_slots = lax.optimization_barrier(
        (tokens, cotangent, old_first, old_second, old_holder, new_owner, chip_slots)
    )
    slots = lax.all_gather(chip_slots, ("z", "x"), axis=0, tiled=True)

    moments = jnp.concatenate([old_first[0].astype(BF16), old_second[0].astype(BF16)], axis=1)
    moments = moments.reshape(4, 2, 2 * SLOTS, 1536)
    chip = jnp.concatenate([of_core(moments, 1), send(of_core(moments, 1, other=True), "c", 1)], axis=1)

    def for_y(shift):
        return lax.dynamic_index_in_dim(chip, (me["y"] + shift) % 4, 0, keepdims=False)

    shard_moments = jnp.concatenate([for_y(0)] + [send(for_y(shift), "y", shift) for shift in SHIFTS], axis=0)

    other_tokens = send(tokens, "c", 1)
    cot_half = cotangent.reshape(512, 2, 384)
    own_cot = of_core(cot_half, 1)
    other_cot = send(of_core(cot_half, 1, other=True), "c", 1)
    pair = jnp.concatenate([tokens, other_tokens], axis=0)

    holder = old_holder[:, 0].reshape(8, 512)
    order = jnp.arange(512, dtype=jnp.int32)
    before = order[None, :] < order[:, None]
    held_rank = jnp.sum(((holder[:, None, :] == holder[:, :, None]) & before[None]).astype(jnp.int32), axis=2)
    within = relative(holder // 2 % 4, me["y"]) * 10 + (holder % 2 != core).astype(jnp.int32) * SLOTS + held_rank
    index = (holder // 8 * 40 + within).reshape(4096, 1)

    my_holder = lax.dynamic_index_in_dim(holder, fsdp_at, 0, keepdims=False)
    my_rank = lax.dynamic_index_in_dim(held_rank, fsdp_at, 0, keepdims=False)
    moment_at = (
        my_holder // 8 * 80
        + relative(my_holder // 2 % 4, me["y"]) * 20
        + (my_holder % 2 != core).astype(jnp.int32) * 10
        + my_rank
    )
    owner = lax.dynamic_index_in_dim(new_owner[:, 0].reshape(8, 512), fsdp_at, 0, keepdims=False)
    own_rank = jnp.sum(((owner[None, :] == owner[:, None]) & before).astype(jnp.int32), axis=1)
    picked = (owner == dp_at)[None, :] & (own_rank[None, :] == jnp.arange(48, dtype=jnp.int32)[:, None])
    own_place = jnp.sum(jnp.where(picked, order[None, :] + 1, 0), axis=1) - 1
    own_at = jnp.sum(jnp.where(picked, moment_at[None, :] + 1, 0), axis=1) - 1
    own_second_at = jnp.where(own_at >= 0, own_at + SLOTS, -1)
    moment_index = jnp.concatenate([moment_at, moment_at + SLOTS, own_at, own_second_at])[:, None]
    own_place = own_place[:, None]

    slots, index, other_tokens, own_cot, other_cot, pair, shard_moments, moment_index, own_place = lax.optimization_barrier(
        (slots, index, other_tokens, own_cot, other_cot, pair, shard_moments, moment_index, own_place)
    )
    all_moments = lax.all_gather(shard_moments, ("z", "x"), axis=0, tiled=True)

    weight, dmixed = forward(index, slots, tokens, other_tokens, own_cot, other_cot)
    grads = [
        lax.dot_general(
            pair, dmixed[:, group * 256 : (group + 1) * 256], (((0,), (0,)), ((), ())), preferred_element_type=F32
        ).astype(BF16)
        for group in range(3)
    ]

    def chunk(value, dim, axis, shift):
        return lax.dynamic_index_in_dim(value, (me[axis] + shift) % 4, dim, keepdims=False)

    values = [grad.reshape(4, 2, 4, 128, 256) for grad in grads]
    plan = ((0, "y"), (2, "z"), (2, "x"))
    own = [chunk(value, dim, axis, 0) for value, (dim, axis) in zip(values, plan)]
    towards = jnp.where(core == 0, 1, 3)
    steps = [
        [chunk(value, dim, axis, shift) for value, (dim, axis) in zip(values, plan)]
        for shift in (towards, 4 - towards, 2)
    ]

    def step(parts, turn):
        return [send_by_core(part, axis, turn) for part, (_, axis) in zip(parts, plan)]

    def together(*groups):
        flat = lax.optimization_barrier(tuple(item for group in groups for item in group))
        out = []
        for group in groups:
            out.append(list(flat[: len(group)]))
            flat = flat[len(group) :]
        return out

    (own, step_a, step_b, step_c, (dmixed, weight)) = together(own, *steps, (dmixed, weight))
    got_a = step(step_a, 1)
    other_part = back(1, dmixed, weight)
    got_a, step_b, step_c, (other_part, weight) = together(got_a, step_b, step_c, (other_part, weight))
    got_b = step(step_b, 3)
    partner_part = send(other_part, "c", 1)
    shard_weight = lax.dynamic_slice_in_dim(weight, me["y"] * 1024, 1024, 0).reshape(2, 512, 768)
    weight_keep = of_core(shard_weight, 0)
    weight_give = of_core(shard_weight, 0, other=True)
    got_b, step_c, (partner_part, weight_keep, weight_give) = together(
        got_b, step_c, (partner_part, weight_keep, weight_give)
    )
    got_c = step(step_c, 2)
    input_grad = back(0, dmixed, weight, partner_part)
    weight_recv = send(weight_give, "c", 1)
    got_c, (input_grad, weight_recv) = together(got_c, (input_grad, weight_recv))
    by_y, by_z, by_x = [
        symmetric_sum(parts).astype(BF16) for parts in zip(own, got_a, got_b, got_c)
    ]

    rest = jnp.concatenate([by_z.reshape(4, 2, 128, 256), by_x.reshape(4, 2, 128, 256)], axis=-1)
    shifts = (0,) + SHIFTS
    parts_y, parts_z = together([chunk(rest, 0, "y", shift) for shift in shifts], [chunk(by_y, 1, "z", shift) for shift in shifts])
    got_y = [send(part, "y", shift) for part, shift in zip(parts_y[1:], SHIFTS)]
    got_z = [send(part, "z", shift) for part, shift in zip(parts_z[1:], SHIFTS)]
    rest = symmetric_sum(parts_y[:1] + got_y).astype(BF16)
    by_y = symmetric_sum(parts_z[:1] + got_z).astype(BF16)

    value = jnp.concatenate([by_y, rest], axis=-1)
    keep = of_core(value, 0)
    recv = send(of_core(value, 0, other=True), "c", 1)
    low = jnp.where(core == 0, keep, recv)
    high = jnp.where(core == 0, recv, keep)
    wide = jnp.concatenate([low[:, :512], high[:, :512]], axis=1)
    narrow = jnp.concatenate([low[:, 512:], high[:, 512:]], axis=1)
    wide, narrow = lax.optimization_barrier((wide, narrow))
    wide = symmetric_sum(gather_axis(wide, "x")).astype(BF16)
    narrow = symmetric_sum(gather_axis(narrow, "z")).astype(BF16)
    wide, narrow, all_moments = lax.optimization_barrier((wide, narrow, all_moments))
    moment_values = moment_rows(moment_index, all_moments)
    place = jnp.stack([me["z"], me["x"]]).astype(jnp.int32)
    wide, narrow, (moment_values,) = together(gather_axis(wide, "z"), gather_axis(narrow, "x"), (moment_values,))
    summed, square = assemble(place, wide, narrow)
    square = square + send(square, "c", 1)
    square = symmetric_sum(gather_axis(square, "y"))
    new_shard, first_out, second_out = adam(
        core.astype(jnp.int32)[None], square, own_place, summed, moment_values, weight_keep, weight_recv
    )
    return (input_grad, new_shard, first_out[None, None], second_out[None, None])


def solution(mesh):
    chips = Mesh(mesh.devices.reshape(4, 4, 4, 2), ("z", "x", "y", "c"))
    every = ("z", "x", "y", "c")
    placed = (
        P(every, None),
        P(every, None),
        P(every, None, None, None),
        P(every, None, None, None),
        P(every, None, None, None),
        P(),
        P(),
    )
    return jax.shard_map(
        on_device,
        mesh=chips,
        in_specs=placed,
        out_specs=(
            P(every, None),
            P(("y", "c"), None),
            P(("y", "c"), ("z", "x"), None, None),
            P(("y", "c"), ("z", "x"), None, None),
        ),
        check_vma=False,
    )
```

```python
import math

import jax
import jax.numpy as jnp
import numpy as np
from jax import lax
from jax.experimental import pallas as pl
from jax.experimental.pallas import tpu as pltpu
from jax.sharding import Mesh
from jax.sharding import PartitionSpec as P

beta_one = 0.9
beta_two = 0.999
learn_rate = 0.01
adam_eps = 1e-08
step_count = 100

SIZE = {"z": 4, "x": 4, "y": 4, "c": 2}
SHIFTS = (1, 3, 2)
OFFSETS = (0, 3, 1, 2)
SLOTS = 5
BF16 = jnp.bfloat16
F32 = jnp.float32


def send(value, axis, shift):
    size = SIZE[axis]
    return lax.ppermute(value, axis, [(i, (i + shift) % size) for i in range(size)])


def send_by_core(value, axis, shift):
    pairs = [(i * 2 + c, (i + (shift if c == 0 else 4 - shift)) % 4 * 2 + c) for i in range(4) for c in range(2)]
    return lax.ppermute(value, (axis, "c"), pairs)


def gather_axis(block, axis):
    return [block] + [send(block, axis, shift) for shift in SHIFTS]


def relative(source, mine):
    away = (source - mine) % 4
    return jnp.where(away == 0, 0, jnp.where(away == 3, 1, jnp.where(away == 1, 2, 3)))


def symmetric_sum(parts):
    own, left, right, across = [part.astype(F32) for part in parts]
    return (own + across) + (left + right)


def pick_rows(index, rows):
    column = jnp.transpose(jnp.broadcast_to(index, (128, index.shape[1])))
    lanes = lax.broadcasted_iota(jnp.int32, column.shape, 1)
    pick = [(column == lanes + at).astype(F32).astype(BF16) for at in range(0, rows.shape[0], 128)]
    return jnp.dot(jnp.concatenate(pick, axis=1), rows, preferred_element_type=F32).astype(BF16)


def params(mib):
    return pltpu.CompilerParams(vmem_limit_bytes=mib * 1024 * 1024)


def cost(macs, moved):
    return pl.CostEstimate(flops=2 * macs, bytes_accessed=moved, transcendentals=0)


def chip_merge_source():
    i = np.arange(320)
    b, chip, core, k = i // 40, i // 10 % 4, i // 5 % 2, i % 5
    return np.pad(chip * 80 + core * 40 + b * 5 + k, (0, 64), constant_values=-1).astype(np.int32)[None]


def chip_merge_kernel(source_ref, a_ref, b_ref, c_ref, d_ref, out_ref, rows_ref):
    for piece, ref in enumerate((a_ref, b_ref, c_ref, d_ref)):
        rows_ref[piece * 80 : (piece + 1) * 80, :] = ref[...]
    rows_ref[320:, :] = jnp.zeros_like(rows_ref[320:, :])
    out_ref[...] = pick_rows(source_ref[...], rows_ref[...])[:320]


def chip_merge(parts):
    columns = parts[0].shape[1]
    return pl.pallas_call(
        chip_merge_kernel,
        out_shape=jax.ShapeDtypeStruct((320, columns), BF16),
        scratch_shapes=[pltpu.VMEM((384, columns), BF16)],
        compiler_params=params(16),
        cost_estimate=cost(320 * 320 * columns, 1_000_000),
    )(jnp.asarray(chip_merge_source()), *parts)


def plane_merge_source():
    i = np.arange(320)
    b, block, j = i // 160, i // 40 % 4, i % 40
    return np.pad(block * 80 + b * 40 + j, (0, 64), constant_values=-1).astype(np.int32)[None]


def plane_merge_kernel(source_ref, a_ref, b_ref, c_ref, d_ref, out_ref, rows_ref):
    rows_ref[320:, :] = jnp.zeros_like(rows_ref[320:, :])
    for pair in range(4):
        for piece, ref in enumerate((a_ref, b_ref, c_ref, d_ref)):
            rows_ref[piece * 80 : (piece + 1) * 80, :] = ref[pair * 80 : (pair + 1) * 80, :]
        out_ref[pair * 320 : (pair + 1) * 320, :] = pick_rows(source_ref[...], rows_ref[...])[:320]


def plane_merge(parts):
    return pl.pallas_call(
        plane_merge_kernel,
        out_shape=jax.ShapeDtypeStruct((1280, 256), BF16),
        scratch_shapes=[pltpu.VMEM((384, 256), BF16)],
        compiler_params=params(16),
        cost_estimate=cost(4 * 320 * 320 * 256, 1_500_000),
    )(jnp.asarray(plane_merge_source()), *parts)


def forward_kernel(
    wide_index_ref, narrow_index_ref, own_ref, other_ref, own_cot_ref, other_cot_ref, wide_ref, a_ref, b_ref, c_ref, d_ref,
    weight_ref, dmixed_ref, acc_ref, wide_rows_ref, narrow_rows_ref,
):
    step = pl.program_id(0)

    @pl.when(step == 0)
    def _():
        acc_ref[...] = jnp.zeros_like(acc_ref)

    for b in range(2):
        for chip in range(16):
            wide_rows_ref[b, chip * 40 : (chip + 1) * 40, :] = wide_ref[chip, b * 40 : (b + 1) * 40, :]
        for piece, ref in enumerate((a_ref, b_ref, c_ref, d_ref)):
            narrow_rows_ref[b, piece * 160 : (piece + 1) * 160, :] = ref[b * 160 : (b + 1) * 160, :]
        shard = pl.ds(step * 2 + b, 1)
        rows = slice(b * 512, (b + 1) * 512)
        weight_ref[rows, :256] = pick_rows(narrow_index_ref[shard, :], narrow_rows_ref[b])
        weight_ref[rows, 256:] = pick_rows(wide_index_ref[shard, :], wide_rows_ref[b])
    acc_ref[:512, :] += jnp.dot(own_ref[...], weight_ref[...], preferred_element_type=F32)
    acc_ref[512:, :] += jnp.dot(other_ref[...], weight_ref[...], preferred_element_type=F32)

    @pl.when(step == 3)
    def _():
        for half, cot_ref in enumerate((own_cot_ref, other_cot_ref)):
            for at_row in range(0, 512, 64):
                rows = slice(half * 512 + at_row, half * 512 + at_row + 64)
                for group in range(3):
                    at = group * 256
                    gate = acc_ref[rows, at : at + 128]
                    up = acc_ref[rows, at + 128 : at + 256]
                    cot = cot_ref[at_row : at_row + 64, group * 128 : (group + 1) * 128].astype(F32)
                    sig = 1.0 / (1.0 + jnp.exp(-gate))
                    dmixed_ref[rows, at : at + 128] = (cot * up * sig * (1.0 + gate * (1.0 - sig))).astype(BF16)
                    dmixed_ref[rows, at + 128 : at + 256] = (cot * gate * sig).astype(BF16)


def forward(wide_index, narrow_index, own, other, own_cot, other_cot, wide, narrow):
    index_spec = pl.BlockSpec((8, 512), lambda i: (0, 0))
    tokens_spec = pl.BlockSpec((512, 1024), lambda i: (0, i))
    cot_spec = pl.BlockSpec((512, 384), lambda i: (0, 0))
    return pl.pallas_call(
        forward_kernel,
        grid=(4,),
        in_specs=[index_spec, index_spec, tokens_spec, tokens_spec, cot_spec, cot_spec]
        + [pl.BlockSpec((16, 80, 512), lambda i: (0, i, 0))]
        + [pl.BlockSpec((320, 256), lambda i: (i, 0))] * 4,
        out_specs=[pl.BlockSpec((1024, 768), lambda i: (i, 0)), pl.BlockSpec((1024, 768), lambda i: (0, 0))],
        out_shape=[jax.ShapeDtypeStruct((4096, 768), BF16), jax.ShapeDtypeStruct((1024, 768), BF16)],
        scratch_shapes=[
            pltpu.VMEM((1024, 768), F32),
            pltpu.VMEM((2, 640, 512), BF16),
            pltpu.VMEM((2, 640, 256), BF16),
        ],
        compiler_params=params(46),
        cost_estimate=cost(1024 * 4096 * 768 + 4096 * 640 * 768, 24_000_000),
    )(wide_index, narrow_index, own, other, own_cot, other_cot, wide, *narrow)


def back_kernel(dmixed_ref, weight_ref, *rest):
    total = lax.dot_general(dmixed_ref[...], weight_ref[...], (((1,), (1,)), ((), ())), preferred_element_type=F32)
    if len(rest) == 2:
        total = total + rest[0][...].astype(F32)
    rest[-1][...] = total.astype(BF16)


def back(half, dmixed, weight, add=None):
    out_spec = pl.BlockSpec((512, 512), lambda b: (0, b))
    specs = [pl.BlockSpec((512, 768), lambda b: (half, 0)), pl.BlockSpec((512, 768), lambda b: (b, 0))]
    extra = []
    if add is not None:
        specs.append(out_spec)
        extra.append(add)
    return pl.pallas_call(
        back_kernel,
        grid=(8,),
        in_specs=specs,
        out_specs=out_spec,
        out_shape=jax.ShapeDtypeStruct((512, 4096), BF16),
        compiler_params=params(32),
        cost_estimate=cost(512 * 4096 * 768, 14_000_000),
    )(dmixed, weight, *extra)


def moment_kernel(index_ref, in_ref, out_ref):
    out_ref[...] = pick_rows(index_ref[...], in_ref[...])


def moment_rows(index, gathered):
    count = index.shape[1]
    return pl.pallas_call(
        moment_kernel,
        grid=(3,),
        in_specs=[pl.BlockSpec((1, count), lambda j: (0, 0)), pl.BlockSpec((1280, 512), lambda j: (0, j))],
        out_specs=pl.BlockSpec((count, 512), lambda j: (0, j)),
        out_shape=jax.ShapeDtypeStruct((count, 1536), BF16),
        compiler_params=params(56),
        cost_estimate=cost(count * 1280 * 1536, 8_000_000),
    )(index, gathered)


def assemble_kernel(place_ref, *refs):
    out_ref, square_ref = refs[8], refs[9]
    for which, groups in enumerate(((0, 1), (2,))):
        for ref, offset in zip(refs[which * 4 : which * 4 + 4], OFFSETS):
            rows = pl.ds(pl.multiple_of(((place_ref[which] + offset) % 4) * 128, 128), 128)
            for core in range(2):
                for nth, group in enumerate(groups):
                    for part in range(2):
                        at = core * 256 * len(groups) + nth * 256 + part * 128
                        to = part * 768 + core * 384 + group * 128
                        out_ref[rows, to : to + 128] = ref[:, at : at + 128]
    total = jnp.zeros((8, 128), F32)
    for step in range(16):
        rows = out_ref[step * 32 : (step + 1) * 32, :].astype(F32)
        total = total + jnp.sum((rows * rows).reshape(4, 8, 12, 128), axis=(0, 2))
    square_ref[...] = total


def assemble(place, left, right):
    vmem = pl.BlockSpec(memory_space=pltpu.VMEM)
    return pl.pallas_call(
        assemble_kernel,
        in_specs=[pl.BlockSpec(memory_space=pltpu.SMEM)] + [vmem] * 8,
        out_specs=[vmem, vmem],
        out_shape=[jax.ShapeDtypeStruct((512, 1536), BF16), jax.ShapeDtypeStruct((8, 128), F32)],
        compiler_params=params(16),
        cost_estimate=cost(0, 3_200_000),
    )(place, *left, *right)


def adam_kernel(core_ref, square_ref, place_ref, grad_ref, moments_ref, *refs):
    keep_refs, recv_refs, (new_ref, first_ref, second_ref) = refs[:3], refs[3:6], refs[6:]
    clip_norm = math.sqrt(4096 * 1536)
    factor = jnp.minimum(1.0, clip_norm / jnp.sqrt(jnp.sum(square_ref[...]) + 1e-06))
    bias_one = 1.0 - beta_one**step_count
    bias_two = 1.0 - beta_two**step_count
    kept = pl.program_id(0) % 2 == core_ref[0]

    step_one = learn_rate / bias_one
    to_first = (1.0 - beta_one) * factor
    to_second = (1.0 - beta_two) * factor * factor

    for group in range(3):
        at = slice(group * 128, (group + 1) * 128)
        for at_row in range(0, 512, 64):
            rows = slice(at_row, at_row + 64)
            grad = grad_ref[rows, at].astype(F32)
            first = moments_ref[rows, at].astype(F32) * (beta_one * step_one) + grad * (to_first * step_one)
            second = moments_ref[512 + at_row : 576 + at_row, at].astype(F32) * (beta_two / bias_two)
            second = second + grad * grad * (to_second / bias_two)
            below = second * lax.rsqrt(second) + adam_eps
            guess = pl.reciprocal(below, approx=True)
            update = first * (guess * (2.0 - below * guess))
            weight = jnp.where(kept, keep_refs[group][rows, :], recv_refs[group][rows, :])
            new_ref[rows, at] = (weight.astype(F32) - update).astype(BF16)
    own_grad = pick_rows(place_ref[...], grad_ref[...])[:48].astype(F32)
    filled = jnp.transpose(jnp.broadcast_to(place_ref[...], (128, 128)))[:48, :1] >= 0
    first_own = beta_one * moments_ref[1024:1072, :].astype(F32) + to_first * own_grad
    second_own = beta_two * moments_ref[1072:1120, :].astype(F32) + (1.0 - beta_two) * (factor * own_grad) * (factor * own_grad)
    first_ref[...] = jnp.where(filled, first_own, 0.0)
    second_ref[...] = jnp.where(filled, second_own, 0.0)


def adam(core, square, place, grad, moments, keep, recv):
    wide = pl.BlockSpec((512, 384), lambda j: (0, j))
    own = pl.BlockSpec((48, 384), lambda j: (0, j))
    weight_specs = [pl.BlockSpec((512, 128), lambda j, group=group: (0, group * 2 + j // 2)) for group in range(3)]
    return pl.pallas_call(
        adam_kernel,
        grid=(4,),
        in_specs=[
            pl.BlockSpec(memory_space=pltpu.SMEM),
            pl.BlockSpec((8, 128), lambda j: (0, 0)),
            pl.BlockSpec((1, 128), lambda j: (0, 0)),
            wide,
            pl.BlockSpec((1152, 384), lambda j: (0, j)),
        ]
        + weight_specs * 2,
        out_specs=[wide, own, own],
        out_shape=[
            jax.ShapeDtypeStruct((512, 1536), BF16),
            jax.ShapeDtypeStruct((48, 1536), F32),
            jax.ShapeDtypeStruct((48, 1536), F32),
        ],
        compiler_params=params(24),
        cost_estimate=cost(48 * 512 * 1536, 9_000_000),
    )(core, square, place, grad, moments, keep, keep, keep, recv, recv, recv)


def on_device(tokens, cotangent, old_weight, old_first, old_second, old_holder, new_owner):
    me = {axis: lax.axis_index(axis) for axis in "zxyc"}
    core = me["c"]
    dp_at = me["z"] * 4 + me["x"]
    fsdp_at = me["y"] * 2 + core

    def of_core(value, axis, other=False):
        return lax.dynamic_index_in_dim(value, 1 - core if other else core, axis, keepdims=False)

    def chunk(value, dim, axis, shift):
        return lax.dynamic_index_in_dim(value, (me[axis] + shift) % 4, dim, keepdims=False)

    def chunks(value, dim, axis):
        return [chunk(value, dim, axis, 0)] + [chunk(value, dim, axis, shift) for shift in SHIFTS]

    def together(*groups):
        flat = lax.optimization_barrier(tuple(item for group in groups for item in group))
        out = []
        for group in groups:
            out.append(list(flat[: len(group)]))
            flat = flat[len(group) :]
        return out

    def total(parts):
        return symmetric_sum(parts).astype(BF16)

    by_half = old_weight[0].reshape(8 * SLOTS, 2, 2, 3, 128).transpose(2, 0, 3, 1, 4).reshape(2, 8 * SLOTS, 768)
    got = send(of_core(by_half, 0, other=True), "c", 1)
    chip_slots = jnp.concatenate([of_core(by_half, 0), got], axis=0)
    narrow_slots, wide_slots = chip_slots[:, :256], chip_slots[:, 256:]
    wide_slots = chip_merge(gather_axis(wide_slots, "y"))
    wide_slots, tokens, cotangent, old_first, old_second, old_holder, new_owner = lax.optimization_barrier(
        (wide_slots, tokens, cotangent, old_first, old_second, old_holder, new_owner)
    )
    wide_slots = lax.all_gather(wide_slots, ("z", "x"), axis=0, tiled=True).reshape(16, 320, 512)
    narrow_slots = chip_merge(gather_axis(narrow_slots, "x"))
    narrow_slots = gather_axis(plane_merge(gather_axis(narrow_slots, "z")), "y")

    moments = jnp.concatenate([old_first[0].astype(BF16), old_second[0].astype(BF16)], axis=1)
    moments = moments.reshape(4, 2, 2 * SLOTS, 1536)
    chip = jnp.concatenate([of_core(moments, 1), send(of_core(moments, 1, other=True), "c", 1)], axis=1)

    def for_y(shift):
        return lax.dynamic_index_in_dim(chip, (me["y"] + shift) % 4, 0, keepdims=False)

    shard_moments = jnp.concatenate([for_y(0)] + [send(for_y(shift), "y", shift) for shift in SHIFTS], axis=0)

    other_tokens = send(tokens, "c", 1)
    cot_half = cotangent.reshape(512, 2, 384)
    own_cot = of_core(cot_half, 1)
    other_cot = send(of_core(cot_half, 1, other=True), "c", 1)
    pair = jnp.concatenate([tokens, other_tokens], axis=0)

    def gradient(dmixed):
        return lax.dot_general(pair, dmixed, (((0,), (0,)), ((), ())), preferred_element_type=F32).astype(BF16)

    holder = old_holder[:, 0].reshape(8, 512)
    order = jnp.arange(512, dtype=jnp.int32)
    before = order[None, :] < order[:, None]
    held_rank = jnp.sum(((holder[:, None, :] == holder[:, :, None]) & before[None]).astype(jnp.int32), axis=2)
    within = (holder % 2 != core).astype(jnp.int32) * SLOTS + held_rank
    rel = {
        "z": relative(holder // 32, me["z"]),
        "x": relative(holder // 8 % 4, me["x"]),
        "y": relative(holder // 2 % 4, me["y"]),
    }
    narrow_index = rel["y"] * 160 + rel["z"] * 40 + rel["x"] * 10 + within
    wide_index = holder // 8 * 40 + rel["y"] * 10 + within

    my_holder = lax.dynamic_index_in_dim(holder, fsdp_at, 0, keepdims=False)
    my_rank = lax.dynamic_index_in_dim(held_rank, fsdp_at, 0, keepdims=False)
    moment_at = (
        my_holder // 8 * 80
        + relative(my_holder // 2 % 4, me["y"]) * 20
        + (my_holder % 2 != core).astype(jnp.int32) * 10
        + my_rank
    )
    owner = lax.dynamic_index_in_dim(new_owner[:, 0].reshape(8, 512), fsdp_at, 0, keepdims=False)
    own_rank = jnp.sum(((owner[None, :] == owner[:, None]) & before).astype(jnp.int32), axis=1)
    picked = (owner == dp_at)[None, :] & (own_rank[None, :] == jnp.arange(128, dtype=jnp.int32)[:, None])
    own_place = jnp.sum(jnp.where(picked, order[None, :] + 1, 0), axis=1) - 1
    own_at = jnp.sum(jnp.where(picked[:48], moment_at[None, :] + 1, 0), axis=1) - 1
    own_second_at = jnp.where(own_at >= 0, own_at + SLOTS, -1)
    none = jnp.full((32,), -1, jnp.int32)
    moment_index = jnp.concatenate([moment_at, moment_at + SLOTS, own_at, own_second_at, none])[None]
    own_place = own_place[None]

    (wide_slots, wide_index, narrow_index, other_tokens, own_cot, other_cot, pair), narrow_slots, (
        shard_moments,
        moment_index,
        own_place,
    ) = together(
        (wide_slots, wide_index, narrow_index, other_tokens, own_cot, other_cot, pair),
        narrow_slots,
        (shard_moments, moment_index, own_place),
    )
    all_moments = lax.all_gather(shard_moments, ("z", "x"), axis=0, tiled=True)
    weight, dmixed = forward(
        wide_index, narrow_index, tokens, other_tokens, own_cot, other_cot, wide_slots, narrow_slots
    )

    grads = [gradient(dmixed[:, group * 256 : (group + 1) * 256]).reshape(4, 2, 4, 128, 256) for group in range(3)]
    plan = ((0, "y"), (2, "z"), (2, "x"))
    own = [chunk(value, dim, axis, 0) for value, (dim, axis) in zip(grads, plan)]
    towards = jnp.where(core == 0, 1, 3)
    turns = [
        [chunk(value, dim, axis, shift) for value, (dim, axis) in zip(grads, plan)]
        for shift in (towards, 4 - towards, 2)
    ]

    def turn(parts, shift):
        return [send_by_core(part, axis, shift) for part, (_, axis) in zip(parts, plan)]

    got_one = turn(turns[0], 1)
    _, (late_dmixed, late_weight) = together(turns[0], (dmixed, weight))
    other_part = back(1, late_dmixed, late_weight)
    got_one, own, turns[1], turns[2], (other_part, late_dmixed, late_weight) = together(
        got_one, own, turns[1], turns[2], (other_part, late_dmixed, late_weight)
    )
    got_two = turn(turns[1], 3)
    partner_part = send(other_part, "c", 1)
    sums = [first.astype(F32) + second.astype(F32) for first, second in zip(own, got_one)]
    shard_weight = lax.dynamic_slice_in_dim(late_weight, me["y"] * 1024, 1024, 0).reshape(2, 512, 768)
    weight_keep = of_core(shard_weight, 0)
    weight_give = of_core(shard_weight, 0, other=True)
    got_two, turns[2], sums, (partner_part, weight_keep, weight_give) = together(
        got_two, turns[2], sums, (partner_part, weight_keep, weight_give)
    )
    got_three = turn(turns[2], 2)
    sums = [part + got.astype(F32) for part, got in zip(sums, got_two)]
    got_three, sums, (weight_give,) = together(got_three, sums, (weight_give,))
    weight_recv = send(weight_give, "c", 1)
    by_y, by_z, by_x = [(part + got.astype(F32)).astype(BF16) for part, got in zip(sums, got_three)]

    rest = jnp.concatenate([by_z.reshape(4, 2, 128, 256), by_x.reshape(4, 2, 128, 256)], axis=-1)
    parts_y, parts_z, (weight_recv,) = together(chunks(rest, 0, "y"), chunks(by_y, 1, "z"), (weight_recv,))
    got_y = [send(part, "y", shift) for part, shift in zip(parts_y[1:], SHIFTS)]
    got_z = [send(part, "z", shift) for part, shift in zip(parts_z[1:], SHIFTS)]
    rest = total(parts_y[:1] + got_y)
    by_y = total(parts_z[:1] + got_z)

    value = jnp.concatenate([by_y, rest], axis=-1)
    keep = of_core(value, 0)
    recv = send(of_core(value, 0, other=True), "c", 1)
    low = jnp.where(core == 0, keep, recv)
    high = jnp.where(core == 0, recv, keep)
    wide = jnp.concatenate([low[:, :512], high[:, :512]], axis=1)
    narrow = jnp.concatenate([low[:, 512:], high[:, 512:]], axis=1)
    wide, narrow, partner_part = lax.optimization_barrier((wide, narrow, partner_part))
    wide = symmetric_sum(gather_axis(wide, "x")).astype(BF16)
    narrow = symmetric_sum(gather_axis(narrow, "z")).astype(BF16)
    input_grad = back(0, late_dmixed, late_weight, partner_part)
    wide, narrow, all_moments, input_grad = lax.optimization_barrier((wide, narrow, all_moments, input_grad))
    moment_values = moment_rows(moment_index, all_moments)
    place = jnp.stack([me["z"], me["x"]]).astype(jnp.int32)
    wide, narrow, (moment_values,) = together(gather_axis(wide, "z"), gather_axis(narrow, "x"), (moment_values,))
    summed, square = assemble(place, wide, narrow)
    square = square + send(square, "c", 1)
    square = symmetric_sum(gather_axis(square, "y"))
    new_shard, first_out, second_out = adam(
        core.astype(jnp.int32)[None], square, own_place, summed, moment_values, weight_keep, weight_recv
    )
    return (input_grad, new_shard, first_out[None, None], second_out[None, None])


def solution(mesh):
    chips = Mesh(mesh.devices.reshape(4, 4, 4, 2), ("z", "x", "y", "c"))
    every = ("z", "x", "y", "c")
    placed = (
        P(every, None),
        P(every, None),
        P(every, None, None, None),
        P(every, None, None, None),
        P(every, None, None, None),
        P(),
        P(),
    )
    return jax.shard_map(
        on_device,
        mesh=chips,
        in_specs=placed,
        out_specs=(
            P(every, None),
            P(("y", "c"), None),
            P(("y", "c"), ("z", "x"), None, None),
            P(("y", "c"), ("z", "x"), None, None),
        ),
        check_vma=False,
    )
```

```python
import math

import jax
import jax.numpy as jnp
import numpy as np
from jax import lax
from jax.experimental import pallas as pl
from jax.experimental.pallas import tpu as pltpu
from jax.sharding import Mesh
from jax.sharding import PartitionSpec as P

beta_one = 0.9
beta_two = 0.999
learn_rate = 0.01
adam_eps = 1e-08
step_count = 100

SIZE = {"z": 4, "x": 4, "y": 4, "c": 2}
SHIFTS = (1, 3, 2)
OFFSETS = (0, 3, 1, 2)
SLOTS = 5
BF16 = jnp.bfloat16
F32 = jnp.float32


def send(value, axis, shift):
    size = SIZE[axis]
    return lax.ppermute(value, axis, [(i, (i + shift) % size) for i in range(size)])


def send_by_core(value, axis, shift):
    pairs = [(i * 2 + c, (i + (shift if c == 0 else 4 - shift)) % 4 * 2 + c) for i in range(4) for c in range(2)]
    return lax.ppermute(value, (axis, "c"), pairs)


def gather_axis(block, axis):
    return [block] + [send(block, axis, shift) for shift in SHIFTS]


def relative(source, mine):
    away = (source - mine) % 4
    return jnp.where(away == 0, 0, jnp.where(away == 3, 1, jnp.where(away == 1, 2, 3)))


def symmetric_sum(parts):
    own, left, right, across = [part.astype(F32) for part in parts]
    return (own + across) + (left + right)


def pick_rows(index, rows):
    column = jnp.transpose(jnp.broadcast_to(index, (128, index.shape[1])))
    lanes = lax.broadcasted_iota(jnp.int32, column.shape, 1)
    pick = [(column == lanes + at).astype(F32).astype(BF16) for at in range(0, rows.shape[0], 128)]
    return jnp.dot(jnp.concatenate(pick, axis=1), rows, preferred_element_type=F32).astype(BF16)


def params(mib):
    return pltpu.CompilerParams(vmem_limit_bytes=mib * 1024 * 1024)


def cost(macs, moved):
    return pl.CostEstimate(flops=2 * macs, bytes_accessed=moved, transcendentals=0)


def chip_merge_source():
    i = np.arange(320)
    b, chip, core, k = i // 40, i // 10 % 4, i // 5 % 2, i % 5
    return np.pad(chip * 80 + core * 40 + b * 5 + k, (0, 64), constant_values=-1).astype(np.int32)[None]


def chip_merge_kernel(source_ref, a_ref, b_ref, c_ref, d_ref, out_ref, rows_ref):
    for piece, ref in enumerate((a_ref, b_ref, c_ref, d_ref)):
        rows_ref[piece * 80 : (piece + 1) * 80, :] = ref[...]
    rows_ref[320:, :] = jnp.zeros_like(rows_ref[320:, :])
    out_ref[...] = pick_rows(source_ref[...], rows_ref[...])[:320]


def chip_merge(parts):
    columns = parts[0].shape[1]
    return pl.pallas_call(
        chip_merge_kernel,
        out_shape=jax.ShapeDtypeStruct((320, columns), BF16),
        scratch_shapes=[pltpu.VMEM((384, columns), BF16)],
        compiler_params=params(16),
        cost_estimate=cost(320 * 320 * columns, 1_000_000),
    )(jnp.asarray(chip_merge_source()), *parts)


def plane_merge_source():
    i = np.arange(320)
    b, block, j = i // 160, i // 40 % 4, i % 40
    return np.pad(block * 80 + b * 40 + j, (0, 64), constant_values=-1).astype(np.int32)[None]


def plane_merge_kernel(source_ref, a_ref, b_ref, c_ref, d_ref, out_ref, rows_ref):
    rows_ref[320:, :] = jnp.zeros_like(rows_ref[320:, :])
    for pair in range(4):
        for piece, ref in enumerate((a_ref, b_ref, c_ref, d_ref)):
            rows_ref[piece * 80 : (piece + 1) * 80, :] = ref[pair * 80 : (pair + 1) * 80, :]
        out_ref[pair * 320 : (pair + 1) * 320, :] = pick_rows(source_ref[...], rows_ref[...])[:320]


def plane_merge(parts):
    return pl.pallas_call(
        plane_merge_kernel,
        out_shape=jax.ShapeDtypeStruct((1280, 256), BF16),
        scratch_shapes=[pltpu.VMEM((384, 256), BF16)],
        compiler_params=params(16),
        cost_estimate=cost(4 * 320 * 320 * 256, 1_500_000),
    )(jnp.asarray(plane_merge_source()), *parts)


def forward_kernel(
    wide_index_ref, narrow_index_ref, own_ref, other_ref, own_cot_ref, other_cot_ref, wide_ref, a_ref, b_ref, c_ref, d_ref,
    weight_ref, dmixed_ref, acc_ref, wide_rows_ref, narrow_rows_ref,
):
    step = pl.program_id(0)

    @pl.when(step == 0)
    def _():
        acc_ref[...] = jnp.zeros_like(acc_ref)

    for b in range(2):
        for chip in range(16):
            wide_rows_ref[b, chip * 40 : (chip + 1) * 40, :] = wide_ref[chip, b * 40 : (b + 1) * 40, :]
        for piece, ref in enumerate((a_ref, b_ref, c_ref, d_ref)):
            narrow_rows_ref[b, piece * 160 : (piece + 1) * 160, :] = ref[b * 160 : (b + 1) * 160, :]
        shard = pl.ds(step * 2 + b, 1)
        rows = slice(b * 512, (b + 1) * 512)
        weight_ref[rows, :256] = pick_rows(narrow_index_ref[shard, :], narrow_rows_ref[b])
        weight_ref[rows, 256:] = pick_rows(wide_index_ref[shard, :], wide_rows_ref[b])
    acc_ref[:512, :] += jnp.dot(own_ref[...], weight_ref[...], preferred_element_type=F32)
    acc_ref[512:, :] += jnp.dot(other_ref[...], weight_ref[...], preferred_element_type=F32)

    @pl.when(step == 3)
    def _():
        for half, cot_ref in enumerate((own_cot_ref, other_cot_ref)):
            for at_row in range(0, 512, 64):
                rows = slice(half * 512 + at_row, half * 512 + at_row + 64)
                for group in range(3):
                    at = group * 256
                    gate = acc_ref[rows, at : at + 128]
                    up = acc_ref[rows, at + 128 : at + 256]
                    cot = cot_ref[at_row : at_row + 64, group * 128 : (group + 1) * 128].astype(F32)
                    sig = 1.0 / (1.0 + jnp.exp(-gate))
                    dmixed_ref[rows, at : at + 128] = (cot * up * sig * (1.0 + gate * (1.0 - sig))).astype(BF16)
                    dmixed_ref[rows, at + 128 : at + 256] = (cot * gate * sig).astype(BF16)


def forward(wide_index, narrow_index, own, other, own_cot, other_cot, wide, narrow):
    index_spec = pl.BlockSpec((8, 512), lambda i: (0, 0))
    tokens_spec = pl.BlockSpec((512, 1024), lambda i: (0, i))
    cot_spec = pl.BlockSpec((512, 384), lambda i: (0, 0))
    return pl.pallas_call(
        forward_kernel,
        grid=(4,),
        in_specs=[index_spec, index_spec, tokens_spec, tokens_spec, cot_spec, cot_spec]
        + [pl.BlockSpec((16, 80, 512), lambda i: (0, i, 0))]
        + [pl.BlockSpec((320, 256), lambda i: (i, 0))] * 4,
        out_specs=[pl.BlockSpec((1024, 768), lambda i: (i, 0)), pl.BlockSpec((1024, 768), lambda i: (0, 0))],
        out_shape=[jax.ShapeDtypeStruct((4096, 768), BF16), jax.ShapeDtypeStruct((1024, 768), BF16)],
        scratch_shapes=[
            pltpu.VMEM((1024, 768), F32),
            pltpu.VMEM((2, 640, 512), BF16),
            pltpu.VMEM((2, 640, 256), BF16),
        ],
        compiler_params=params(50),
        cost_estimate=cost(1024 * 4096 * 768 + 4096 * 640 * 768, 24_000_000),
    )(wide_index, narrow_index, own, other, own_cot, other_cot, wide, *narrow)


def back_kernel(dmixed_ref, weight_ref, *rest):
    total = lax.dot_general(dmixed_ref[...], weight_ref[...], (((1,), (1,)), ((), ())), preferred_element_type=F32)
    if len(rest) == 2:
        total = total + rest[0][...].astype(F32)
    rest[-1][...] = total.astype(BF16)


def back(half, dmixed, weight, add=None):
    out_spec = pl.BlockSpec((512, 512), lambda b: (0, b))
    specs = [pl.BlockSpec((512, 768), lambda b: (half, 0)), pl.BlockSpec((512, 768), lambda b: (b, 0))]
    extra = []
    if add is not None:
        specs.append(out_spec)
        extra.append(add)
    return pl.pallas_call(
        back_kernel,
        grid=(8,),
        in_specs=specs,
        out_specs=out_spec,
        out_shape=jax.ShapeDtypeStruct((512, 4096), BF16),
        compiler_params=params(32),
        cost_estimate=cost(512 * 4096 * 768, 14_000_000),
    )(dmixed, weight, *extra)


def moment_kernel(index_ref, in_ref, out_ref):
    out_ref[...] = pick_rows(index_ref[...], in_ref[...])


def moment_rows(index, gathered):
    count = index.shape[1]
    return pl.pallas_call(
        moment_kernel,
        grid=(3,),
        in_specs=[pl.BlockSpec((1, count), lambda j: (0, 0)), pl.BlockSpec((1280, 512), lambda j: (0, j))],
        out_specs=pl.BlockSpec((count, 512), lambda j: (0, j)),
        out_shape=jax.ShapeDtypeStruct((count, 1536), BF16),
        compiler_params=params(28),
        cost_estimate=cost(count * 1280 * 1536, 8_000_000),
    )(index, gathered)


def assemble_kernel(place_ref, *refs):
    out_ref, square_ref = refs[8], refs[9]
    for which, groups in enumerate(((0, 1), (2,))):
        for ref, offset in zip(refs[which * 4 : which * 4 + 4], OFFSETS):
            rows = pl.ds(pl.multiple_of(((place_ref[which] + offset) % 4) * 128, 128), 128)
            for core in range(2):
                for nth, group in enumerate(groups):
                    for part in range(2):
                        at = core * 256 * len(groups) + nth * 256 + part * 128
                        to = part * 768 + core * 384 + group * 128
                        out_ref[rows, to : to + 128] = ref[:, at : at + 128]
    total = jnp.zeros((8, 128), F32)
    for step in range(16):
        rows = out_ref[step * 32 : (step + 1) * 32, :].astype(F32)
        total = total + jnp.sum((rows * rows).reshape(4, 8, 12, 128), axis=(0, 2))
    square_ref[...] = total


def assemble(place, left, right):
    vmem = pl.BlockSpec(memory_space=pltpu.VMEM)
    return pl.pallas_call(
        assemble_kernel,
        in_specs=[pl.BlockSpec(memory_space=pltpu.SMEM)] + [vmem] * 8,
        out_specs=[vmem, vmem],
        out_shape=[jax.ShapeDtypeStruct((512, 1536), BF16), jax.ShapeDtypeStruct((8, 128), F32)],
        compiler_params=params(16),
        cost_estimate=cost(0, 3_200_000),
    )(place, *left, *right)


def adam_kernel(core_ref, square_ref, place_ref, grad_ref, moments_ref, *refs):
    keep_refs, recv_refs, (new_ref, first_ref, second_ref) = refs[:3], refs[3:6], refs[6:]
    clip_norm = math.sqrt(4096 * 1536)
    factor = jnp.minimum(1.0, clip_norm / jnp.sqrt(jnp.sum(square_ref[...]) + 1e-06))
    bias_one = 1.0 - beta_one**step_count
    bias_two = 1.0 - beta_two**step_count
    kept = pl.program_id(0) % 2 == core_ref[0]

    step_one = learn_rate / bias_one
    to_first = (1.0 - beta_one) * factor
    to_second = (1.0 - beta_two) * factor * factor

    for group in range(3):
        at = slice(group * 128, (group + 1) * 128)
        for at_row in range(0, 512, 64):
            rows = slice(at_row, at_row + 64)
            grad = grad_ref[rows, at].astype(F32)
            first = moments_ref[rows, at].astype(F32) * (beta_one * step_one) + grad * (to_first * step_one)
            second = moments_ref[512 + at_row : 576 + at_row, at].astype(F32) * (beta_two / bias_two)
            second = second + grad * grad * (to_second / bias_two)
            below = second * lax.rsqrt(second) + adam_eps
            guess = pl.reciprocal(below, approx=True)
            update = first * (guess * (2.0 - below * guess))
            weight = jnp.where(kept, keep_refs[group][rows, :], recv_refs[group][rows, :])
            new_ref[rows, at] = (weight.astype(F32) - update).astype(BF16)
    own_grad = pick_rows(place_ref[...], grad_ref[...])[:48].astype(F32)
    filled = jnp.transpose(jnp.broadcast_to(place_ref[...], (128, 128)))[:48, :1] >= 0
    first_own = beta_one * moments_ref[1024:1072, :].astype(F32) + to_first * own_grad
    second_own = beta_two * moments_ref[1072:1120, :].astype(F32) + (1.0 - beta_two) * (factor * own_grad) * (factor * own_grad)
    first_ref[...] = jnp.where(filled, first_own, 0.0)
    second_ref[...] = jnp.where(filled, second_own, 0.0)


def adam(core, square, place, grad, moments, keep, recv):
    wide = pl.BlockSpec((512, 384), lambda j: (0, j))
    own = pl.BlockSpec((48, 384), lambda j: (0, j))
    weight_specs = [pl.BlockSpec((512, 128), lambda j, group=group: (0, group * 2 + j // 2)) for group in range(3)]
    return pl.pallas_call(
        adam_kernel,
        grid=(4,),
        in_specs=[
            pl.BlockSpec(memory_space=pltpu.SMEM),
            pl.BlockSpec((8, 128), lambda j: (0, 0)),
            pl.BlockSpec((1, 128), lambda j: (0, 0)),
            wide,
            pl.BlockSpec((1152, 384), lambda j: (0, j)),
        ]
        + weight_specs * 2,
        out_specs=[wide, own, own],
        out_shape=[
            jax.ShapeDtypeStruct((512, 1536), BF16),
            jax.ShapeDtypeStruct((48, 1536), F32),
            jax.ShapeDtypeStruct((48, 1536), F32),
        ],
        compiler_params=params(24),
        cost_estimate=cost(48 * 512 * 1536, 9_000_000),
    )(core, square, place, grad, moments, keep, keep, keep, recv, recv, recv)


def on_device(tokens, cotangent, old_weight, old_first, old_second, old_holder, new_owner):
    me = {axis: lax.axis_index(axis) for axis in "zxyc"}
    core = me["c"]
    dp_at = me["z"] * 4 + me["x"]
    fsdp_at = me["y"] * 2 + core

    def of_core(value, axis, other=False):
        return lax.dynamic_index_in_dim(value, 1 - core if other else core, axis, keepdims=False)

    def chunk(value, dim, axis, shift):
        return lax.dynamic_index_in_dim(value, (me[axis] + shift) % 4, dim, keepdims=False)

    def chunks(value, dim, axis):
        return [chunk(value, dim, axis, 0)] + [chunk(value, dim, axis, shift) for shift in SHIFTS]

    def together(*groups):
        flat = lax.optimization_barrier(tuple(item for group in groups for item in group))
        out = []
        for group in groups:
            out.append(list(flat[: len(group)]))
            flat = flat[len(group) :]
        return out

    def total(parts):
        return symmetric_sum(parts).astype(BF16)

    by_half = old_weight[0].reshape(8 * SLOTS, 2, 2, 3, 128).transpose(2, 0, 3, 1, 4).reshape(2, 8 * SLOTS, 768)
    got = send(of_core(by_half, 0, other=True), "c", 1)
    chip_slots = jnp.concatenate([of_core(by_half, 0), got], axis=0)
    narrow_slots, wide_slots = chip_slots[:, :256], chip_slots[:, 256:]
    wide_slots = chip_merge(gather_axis(wide_slots, "y"))
    wide_slots, tokens, cotangent, old_first, old_second, old_holder, new_owner = lax.optimization_barrier(
        (wide_slots, tokens, cotangent, old_first, old_second, old_holder, new_owner)
    )
    wide_slots = lax.all_gather(wide_slots, ("z", "x"), axis=0, tiled=True).reshape(16, 320, 512)
    narrow_slots = chip_merge(gather_axis(narrow_slots, "x"))
    narrow_slots = gather_axis(plane_merge(gather_axis(narrow_slots, "z")), "y")

    moments = jnp.concatenate([old_first[0].astype(BF16), old_second[0].astype(BF16)], axis=1)
    moments = moments.reshape(4, 2, 2 * SLOTS, 1536)
    chip = jnp.concatenate([of_core(moments, 1), send(of_core(moments, 1, other=True), "c", 1)], axis=1)

    def for_y(shift):
        return lax.dynamic_index_in_dim(chip, (me["y"] + shift) % 4, 0, keepdims=False)

    shard_moments = jnp.concatenate([for_y(0)] + [send(for_y(shift), "y", shift) for shift in SHIFTS], axis=0)

    other_tokens = send(tokens, "c", 1)
    cot_half = cotangent.reshape(512, 2, 384)
    own_cot = of_core(cot_half, 1)
    other_cot = send(of_core(cot_half, 1, other=True), "c", 1)
    pair = jnp.concatenate([tokens, other_tokens], axis=0)

    def gradient(dmixed):
        return lax.dot_general(pair, dmixed, (((0,), (0,)), ((), ())), preferred_element_type=F32).astype(BF16)

    holder = old_holder[:, 0].reshape(8, 512)
    order = jnp.arange(512, dtype=jnp.int32)
    before = order[None, :] < order[:, None]
    held_rank = jnp.sum(((holder[:, None, :] == holder[:, :, None]) & before[None]).astype(jnp.int32), axis=2)
    within = (holder % 2 != core).astype(jnp.int32) * SLOTS + held_rank
    rel = {
        "z": relative(holder // 32, me["z"]),
        "x": relative(holder // 8 % 4, me["x"]),
        "y": relative(holder // 2 % 4, me["y"]),
    }
    narrow_index = rel["y"] * 160 + rel["z"] * 40 + rel["x"] * 10 + within
    wide_index = holder // 8 * 40 + rel["y"] * 10 + within

    my_holder = lax.dynamic_index_in_dim(holder, fsdp_at, 0, keepdims=False)
    my_rank = lax.dynamic_index_in_dim(held_rank, fsdp_at, 0, keepdims=False)
    moment_at = (
        my_holder // 8 * 80
        + relative(my_holder // 2 % 4, me["y"]) * 20
        + (my_holder % 2 != core).astype(jnp.int32) * 10
        + my_rank
    )
    owner = lax.dynamic_index_in_dim(new_owner[:, 0].reshape(8, 512), fsdp_at, 0, keepdims=False)
    own_rank = jnp.sum(((owner[None, :] == owner[:, None]) & before).astype(jnp.int32), axis=1)
    picked = (owner == dp_at)[None, :] & (own_rank[None, :] == jnp.arange(128, dtype=jnp.int32)[:, None])
    own_place = jnp.sum(jnp.where(picked, order[None, :] + 1, 0), axis=1) - 1
    own_at = jnp.sum(jnp.where(picked[:48], moment_at[None, :] + 1, 0), axis=1) - 1
    own_second_at = jnp.where(own_at >= 0, own_at + SLOTS, -1)
    none = jnp.full((32,), -1, jnp.int32)
    moment_index = jnp.concatenate([moment_at, moment_at + SLOTS, own_at, own_second_at, none])[None]
    own_place = own_place[None]

    (wide_slots, wide_index, narrow_index, other_tokens, own_cot, other_cot, pair), narrow_slots, (
        shard_moments,
        moment_index,
        own_place,
    ) = together(
        (wide_slots, wide_index, narrow_index, other_tokens, own_cot, other_cot, pair),
        narrow_slots,
        (shard_moments, moment_index, own_place),
    )
    all_moments = lax.all_gather(shard_moments, ("z", "x"), axis=0, tiled=True)
    weight, dmixed = forward(
        wide_index, narrow_index, tokens, other_tokens, own_cot, other_cot, wide_slots, narrow_slots
    )

    grads = [gradient(dmixed[:, group * 256 : (group + 1) * 256]).reshape(4, 2, 4, 128, 256) for group in range(3)]
    plan = ((0, "y"), (2, "z"), (2, "x"))
    own = [chunk(value, dim, axis, 0) for value, (dim, axis) in zip(grads, plan)]
    towards = jnp.where(core == 0, 1, 3)
    turns = [
        [chunk(value, dim, axis, shift) for value, (dim, axis) in zip(grads, plan)]
        for shift in (2, 4 - towards, towards)
    ]

    def turn(parts, shift):
        return [send_by_core(part, axis, shift) for part, (_, axis) in zip(parts, plan)]

    got_one = turn(turns[0], 1)
    _, (late_dmixed, late_weight) = together(turns[0], (dmixed, weight))
    other_part = back(1, late_dmixed, late_weight)
    got_one, own, turns[1], turns[2], (other_part, late_dmixed, late_weight) = together(
        got_one, own, turns[1], turns[2], (other_part, late_dmixed, late_weight)
    )
    got_two = turn(turns[1], 3)
    partner_part = send(other_part, "c", 1)
    turns[2] = [(part.astype(F32) + got.astype(F32)).astype(BF16) for part, got in zip(turns[2], got_one)]
    shard_weight = lax.dynamic_slice_in_dim(late_weight, me["y"] * 1024, 1024, 0).reshape(2, 512, 768)
    weight_keep = of_core(shard_weight, 0)
    weight_give = of_core(shard_weight, 0, other=True)
    got_two, turns[2], own, (partner_part, weight_keep, weight_give) = together(
        got_two, turns[2], own, (partner_part, weight_keep, weight_give)
    )
    got_three = turn(turns[2], 1)
    sums = [part.astype(F32) + got.astype(F32) for part, got in zip(own, got_two)]
    got_three, sums, (weight_give,) = together(got_three, sums, (weight_give,))
    weight_recv = send(weight_give, "c", 1)
    by_y, by_z, by_x = [(part + got.astype(F32)).astype(BF16) for part, got in zip(sums, got_three)]

    rest = jnp.concatenate([by_z.reshape(4, 2, 128, 256), by_x.reshape(4, 2, 128, 256)], axis=-1)
    parts_y, parts_z, (weight_recv,) = together(chunks(rest, 0, "y"), chunks(by_y, 1, "z"), (weight_recv,))
    got_y = [send(part, "y", shift) for part, shift in zip(parts_y[1:], SHIFTS)]
    got_z = [send(part, "z", shift) for part, shift in zip(parts_z[1:], SHIFTS)]
    rest = total(parts_y[:1] + got_y)
    by_y = total(parts_z[:1] + got_z)

    value = jnp.concatenate([by_y, rest], axis=-1)
    keep = of_core(value, 0)
    recv = send(of_core(value, 0, other=True), "c", 1)
    low = jnp.where(core == 0, keep, recv)
    high = jnp.where(core == 0, recv, keep)
    wide = jnp.concatenate([low[:, :512], high[:, :512]], axis=1)
    narrow = jnp.concatenate([low[:, 512:], high[:, 512:]], axis=1)
    wide, narrow, partner_part = lax.optimization_barrier((wide, narrow, partner_part))
    wide = symmetric_sum(gather_axis(wide, "x")).astype(BF16)
    narrow = symmetric_sum(gather_axis(narrow, "z")).astype(BF16)
    input_grad = back(0, late_dmixed, late_weight, partner_part)
    wide, narrow, all_moments, input_grad = lax.optimization_barrier((wide, narrow, all_moments, input_grad))
    moment_values = moment_rows(moment_index, all_moments)
    place = jnp.stack([me["z"], me["x"]]).astype(jnp.int32)
    wide, narrow, (moment_values,) = together(gather_axis(wide, "z"), gather_axis(narrow, "x"), (moment_values,))
    summed, square = assemble(place, wide, narrow)
    square = square + send(square, "c", 1)
    square = symmetric_sum(gather_axis(square, "y"))
    new_shard, first_out, second_out = adam(
        core.astype(jnp.int32)[None], square, own_place, summed, moment_values, weight_keep, weight_recv
    )
    return (input_grad, new_shard, first_out[None, None], second_out[None, None])


def solution(mesh):
    chips = Mesh(mesh.devices.reshape(4, 4, 4, 2), ("z", "x", "y", "c"))
    every = ("z", "x", "y", "c")
    placed = (
        P(every, None),
        P(every, None),
        P(every, None, None, None),
        P(every, None, None, None),
        P(every, None, None, None),
        P(),
        P(),
    )
    return jax.shard_map(
        on_device,
        mesh=chips,
        in_specs=placed,
        out_specs=(
            P(every, None),
            P(("y", "c"), None),
            P(("y", "c"), ("z", "x"), None, None),
            P(("y", "c"), ("z", "x"), None, None),
        ),
        check_vma=False,
    )
```

```python
import math

import jax
import jax.numpy as jnp
import numpy as np
from jax import lax
from jax.experimental import pallas as pl
from jax.experimental.pallas import tpu as pltpu
from jax.sharding import Mesh
from jax.sharding import PartitionSpec as P

beta_one = 0.9
beta_two = 0.999
learn_rate = 0.01
adam_eps = 1e-08
step_count = 100

SIZE = {"z": 4, "x": 4, "y": 4, "c": 2}
SHIFTS = (1, 3, 2)
OFFSETS = (0, 3, 1, 2)
SLOTS = 5
BF16 = jnp.bfloat16
F32 = jnp.float32


def send(value, axis, shift):
    size = SIZE[axis]
    return lax.ppermute(value, axis, [(i, (i + shift) % size) for i in range(size)])


def send_by_core(value, axis, shift):
    pairs = [(i * 2 + c, (i + (shift if c == 0 else 4 - shift)) % 4 * 2 + c) for i in range(4) for c in range(2)]
    return lax.ppermute(value, (axis, "c"), pairs)


def gather_axis(block, axis):
    return [block] + [send(block, axis, shift) for shift in SHIFTS]


def relative(source, mine):
    away = (source - mine) % 4
    return jnp.where(away == 0, 0, jnp.where(away == 3, 1, jnp.where(away == 1, 2, 3)))


def symmetric_sum(parts):
    own, left, right, across = [part.astype(F32) for part in parts]
    return (own + across) + (left + right)


def pick_rows(index, rows):
    column = jnp.transpose(jnp.broadcast_to(index, (128, index.shape[1])))
    lanes = lax.broadcasted_iota(jnp.int32, column.shape, 1)
    pick = [(column == lanes + at).astype(F32).astype(BF16) for at in range(0, rows.shape[0], 128)]
    return jnp.dot(jnp.concatenate(pick, axis=1), rows, preferred_element_type=F32).astype(BF16)


def params(mib):
    return pltpu.CompilerParams(vmem_limit_bytes=mib * 1024 * 1024)


def cost(macs, moved):
    return pl.CostEstimate(flops=2 * macs, bytes_accessed=moved, transcendentals=0)


def chip_merge_source():
    i = np.arange(320)
    b, chip, core, k = i // 40, i // 10 % 4, i // 5 % 2, i % 5
    return np.pad(chip * 80 + core * 40 + b * 5 + k, (0, 64), constant_values=-1).astype(np.int32)[None]


def chip_merge_kernel(source_ref, a_ref, b_ref, c_ref, d_ref, out_ref, rows_ref):
    for piece, ref in enumerate((a_ref, b_ref, c_ref, d_ref)):
        rows_ref[piece * 80 : (piece + 1) * 80, :] = ref[...]
    rows_ref[320:, :] = jnp.zeros_like(rows_ref[320:, :])
    out_ref[...] = pick_rows(source_ref[...], rows_ref[...])[:320]


def chip_merge(parts):
    columns = parts[0].shape[1]
    return pl.pallas_call(
        chip_merge_kernel,
        out_shape=jax.ShapeDtypeStruct((320, columns), BF16),
        scratch_shapes=[pltpu.VMEM((384, columns), BF16)],
        compiler_params=params(16),
        cost_estimate=cost(320 * 320 * columns, 1_000_000),
    )(jnp.asarray(chip_merge_source()), *parts)


def plane_merge_source():
    i = np.arange(320)
    b, block, j = i // 160, i // 40 % 4, i % 40
    return np.pad(block * 80 + b * 40 + j, (0, 64), constant_values=-1).astype(np.int32)[None]


def plane_merge_kernel(source_ref, a_ref, b_ref, c_ref, d_ref, out_ref, rows_ref):
    rows_ref[320:, :] = jnp.zeros_like(rows_ref[320:, :])
    for pair in range(4):
        for piece, ref in enumerate((a_ref, b_ref, c_ref, d_ref)):
            rows_ref[piece * 80 : (piece + 1) * 80, :] = ref[pair * 80 : (pair + 1) * 80, :]
        out_ref[pair * 320 : (pair + 1) * 320, :] = pick_rows(source_ref[...], rows_ref[...])[:320]


def plane_merge(parts):
    return pl.pallas_call(
        plane_merge_kernel,
        out_shape=jax.ShapeDtypeStruct((1280, 256), BF16),
        scratch_shapes=[pltpu.VMEM((384, 256), BF16)],
        compiler_params=params(16),
        cost_estimate=cost(4 * 320 * 320 * 256, 1_500_000),
    )(jnp.asarray(plane_merge_source()), *parts)


def forward_kernel(
    wide_index_ref, narrow_index_ref, own_ref, other_ref, own_cot_ref, other_cot_ref, wide_ref, a_ref, b_ref, c_ref, d_ref,
    weight_ref, dmixed_ref, acc_ref, wide_rows_ref, narrow_rows_ref,
):
    step = pl.program_id(0)

    @pl.when(step == 0)
    def _():
        acc_ref[...] = jnp.zeros_like(acc_ref)

    for b in range(2):
        for chip in range(16):
            wide_rows_ref[b, chip * 40 : (chip + 1) * 40, :] = wide_ref[chip, b * 40 : (b + 1) * 40, :]
        for piece, ref in enumerate((a_ref, b_ref, c_ref, d_ref)):
            narrow_rows_ref[b, piece * 160 : (piece + 1) * 160, :] = ref[b * 160 : (b + 1) * 160, :]
        shard = pl.ds(step * 2 + b, 1)
        rows = slice(b * 512, (b + 1) * 512)
        weight_ref[rows, :256] = pick_rows(narrow_index_ref[shard, :], narrow_rows_ref[b])
        weight_ref[rows, 256:] = pick_rows(wide_index_ref[shard, :], wide_rows_ref[b])
    acc_ref[:512, :] += jnp.dot(own_ref[...], weight_ref[...], preferred_element_type=F32)
    acc_ref[512:, :] += jnp.dot(other_ref[...], weight_ref[...], preferred_element_type=F32)

    @pl.when(step == 3)
    def _():
        for half, cot_ref in enumerate((own_cot_ref, other_cot_ref)):
            for at_row in range(0, 512, 64):
                rows = slice(half * 512 + at_row, half * 512 + at_row + 64)
                for group in range(3):
                    at = group * 256
                    gate = acc_ref[rows, at : at + 128]
                    up = acc_ref[rows, at + 128 : at + 256]
                    cot = cot_ref[at_row : at_row + 64, group * 128 : (group + 1) * 128].astype(F32)
                    sig = 1.0 / (1.0 + jnp.exp(-gate))
                    dmixed_ref[rows, at : at + 128] = (cot * up * sig * (1.0 + gate * (1.0 - sig))).astype(BF16)
                    dmixed_ref[rows, at + 128 : at + 256] = (cot * gate * sig).astype(BF16)


def forward(wide_index, narrow_index, own, other, own_cot, other_cot, wide, narrow):
    index_spec = pl.BlockSpec((8, 512), lambda i: (0, 0))
    tokens_spec = pl.BlockSpec((512, 1024), lambda i: (0, i))
    cot_spec = pl.BlockSpec((512, 384), lambda i: (0, 0))
    return pl.pallas_call(
        forward_kernel,
        grid=(4,),
        in_specs=[index_spec, index_spec, tokens_spec, tokens_spec, cot_spec, cot_spec]
        + [pl.BlockSpec((16, 80, 512), lambda i: (0, i, 0))]
        + [pl.BlockSpec((320, 256), lambda i: (i, 0))] * 4,
        out_specs=[pl.BlockSpec((1024, 768), lambda i: (i, 0)), pl.BlockSpec((1024, 768), lambda i: (0, 0))],
        out_shape=[jax.ShapeDtypeStruct((4096, 768), BF16), jax.ShapeDtypeStruct((1024, 768), BF16)],
        scratch_shapes=[
            pltpu.VMEM((1024, 768), F32),
            pltpu.VMEM((2, 640, 512), BF16),
            pltpu.VMEM((2, 640, 256), BF16),
        ],
        compiler_params=params(50),
        cost_estimate=cost(1024 * 4096 * 768 + 4096 * 640 * 768, 24_000_000),
    )(wide_index, narrow_index, own, other, own_cot, other_cot, wide, *narrow)


def back_kernel(dmixed_ref, weight_ref, *rest):
    total = lax.dot_general(dmixed_ref[...], weight_ref[...], (((1,), (1,)), ((), ())), preferred_element_type=F32)
    if len(rest) == 2:
        total = total + rest[0][...].astype(F32)
    rest[-1][...] = total.astype(BF16)


def back(half, dmixed, weight, add=None):
    out_spec = pl.BlockSpec((512, 512), lambda b: (0, b))
    specs = [pl.BlockSpec((512, 768), lambda b: (half, 0)), pl.BlockSpec((512, 768), lambda b: (b, 0))]
    extra = []
    if add is not None:
        specs.append(out_spec)
        extra.append(add)
    return pl.pallas_call(
        back_kernel,
        grid=(8,),
        in_specs=specs,
        out_specs=out_spec,
        out_shape=jax.ShapeDtypeStruct((512, 4096), BF16),
        compiler_params=params(32),
        cost_estimate=cost(512 * 4096 * 768, 14_000_000),
    )(dmixed, weight, *extra)


def moment_kernel(index_ref, in_ref, out_ref):
    out_ref[...] = pick_rows(index_ref[...], in_ref[...])


def moment_rows(index, gathered):
    count = index.shape[1]
    return pl.pallas_call(
        moment_kernel,
        grid=(3,),
        in_specs=[pl.BlockSpec((1, count), lambda j: (0, 0)), pl.BlockSpec((1280, 512), lambda j: (0, j))],
        out_specs=pl.BlockSpec((count, 512), lambda j: (0, j)),
        out_shape=jax.ShapeDtypeStruct((count, 1536), BF16),
        compiler_params=params(28),
        cost_estimate=cost(count * 1280 * 1536, 8_000_000),
    )(index, gathered)


def assemble_kernel(place_ref, *refs):
    out_ref, square_ref = refs[8], refs[9]
    for which, groups in enumerate(((0, 1), (2,))):
        for ref, offset in zip(refs[which * 4 : which * 4 + 4], OFFSETS):
            rows = pl.ds(pl.multiple_of(((place_ref[which] + offset) % 4) * 128, 128), 128)
            for core in range(2):
                for nth, group in enumerate(groups):
                    for part in range(2):
                        at = core * 256 * len(groups) + nth * 256 + part * 128
                        to = part * 768 + core * 384 + group * 128
                        out_ref[rows, to : to + 128] = ref[:, at : at + 128]
    total = jnp.zeros((8, 128), F32)
    for step in range(16):
        rows = out_ref[step * 32 : (step + 1) * 32, :].astype(F32)
        total = total + jnp.sum((rows * rows).reshape(4, 8, 12, 128), axis=(0, 2))
    square_ref[...] = total


def assemble(place, left, right):
    vmem = pl.BlockSpec(memory_space=pltpu.VMEM)
    return pl.pallas_call(
        assemble_kernel,
        in_specs=[pl.BlockSpec(memory_space=pltpu.SMEM)] + [vmem] * 8,
        out_specs=[vmem, vmem],
        out_shape=[jax.ShapeDtypeStruct((512, 1536), BF16), jax.ShapeDtypeStruct((8, 128), F32)],
        compiler_params=params(16),
        cost_estimate=cost(0, 3_200_000),
    )(place, *left, *right)


def adam_kernel(core_ref, square_ref, place_ref, grad_ref, moments_ref, *refs):
    keep_refs, recv_refs, (new_ref, first_ref, second_ref) = refs[:3], refs[3:6], refs[6:]
    clip_norm = math.sqrt(4096 * 1536)
    factor = jnp.minimum(1.0, clip_norm / jnp.sqrt(jnp.sum(square_ref[...]) + 1e-06))
    bias_one = 1.0 - beta_one**step_count
    bias_two = 1.0 - beta_two**step_count
    kept = pl.program_id(0) % 2 == core_ref[0]

    step_one = learn_rate / bias_one
    to_first = (1.0 - beta_one) * factor
    to_second = (1.0 - beta_two) * factor * factor

    for group in range(3):
        at = slice(group * 128, (group + 1) * 128)
        for at_row in range(0, 512, 64):
            rows = slice(at_row, at_row + 64)
            grad = grad_ref[rows, at].astype(F32)
            first = moments_ref[rows, at].astype(F32) * (beta_one * step_one) + grad * (to_first * step_one)
            second = moments_ref[512 + at_row : 576 + at_row, at].astype(F32) * (beta_two / bias_two)
            second = second + grad * grad * (to_second / bias_two)
            below = second * lax.rsqrt(second) + adam_eps
            guess = pl.reciprocal(below, approx=True)
            update = first * (guess * (2.0 - below * guess))
            weight = jnp.where(kept, keep_refs[group][rows, :], recv_refs[group][rows, :])
            new_ref[rows, at] = (weight.astype(F32) - update).astype(BF16)
    own_grad = pick_rows(place_ref[...], grad_ref[...])[:48].astype(F32)
    filled = jnp.transpose(jnp.broadcast_to(place_ref[...], (128, 128)))[:48, :1] >= 0
    first_own = beta_one * moments_ref[1024:1072, :].astype(F32) + to_first * own_grad
    second_own = beta_two * moments_ref[1072:1120, :].astype(F32) + (1.0 - beta_two) * (factor * own_grad) * (factor * own_grad)
    first_ref[...] = jnp.where(filled, first_own, 0.0)
    second_ref[...] = jnp.where(filled, second_own, 0.0)


def adam(core, square, place, grad, moments, keep, recv):
    wide = pl.BlockSpec((512, 384), lambda j: (0, j))
    own = pl.BlockSpec((48, 384), lambda j: (0, j))
    weight_specs = [pl.BlockSpec((512, 128), lambda j, group=group: (0, group * 2 + j // 2)) for group in range(3)]
    return pl.pallas_call(
        adam_kernel,
        grid=(4,),
        in_specs=[
            pl.BlockSpec(memory_space=pltpu.SMEM),
            pl.BlockSpec((8, 128), lambda j: (0, 0)),
            pl.BlockSpec((1, 128), lambda j: (0, 0)),
            wide,
            pl.BlockSpec((1152, 384), lambda j: (0, j)),
        ]
        + weight_specs * 2,
        out_specs=[wide, own, own],
        out_shape=[
            jax.ShapeDtypeStruct((512, 1536), BF16),
            jax.ShapeDtypeStruct((48, 1536), F32),
            jax.ShapeDtypeStruct((48, 1536), F32),
        ],
        compiler_params=params(24),
        cost_estimate=cost(48 * 512 * 1536, 9_000_000),
    )(core, square, place, grad, moments, keep, keep, keep, recv, recv, recv)


def on_device(tokens, cotangent, old_weight, old_first, old_second, old_holder, new_owner):
    me = {axis: lax.axis_index(axis) for axis in "zxyc"}
    core = me["c"]
    dp_at = me["z"] * 4 + me["x"]
    fsdp_at = me["y"] * 2 + core

    def of_core(value, axis, other=False):
        return lax.dynamic_index_in_dim(value, 1 - core if other else core, axis, keepdims=False)

    def chunk(value, dim, axis, shift):
        return lax.dynamic_index_in_dim(value, (me[axis] + shift) % 4, dim, keepdims=False)

    def chunks(value, dim, axis):
        return [chunk(value, dim, axis, 0)] + [chunk(value, dim, axis, shift) for shift in SHIFTS]

    def together(*groups):
        flat = lax.optimization_barrier(tuple(item for group in groups for item in group))
        out = []
        for group in groups:
            out.append(list(flat[: len(group)]))
            flat = flat[len(group) :]
        return out

    def total(parts):
        return symmetric_sum(parts).astype(BF16)

    by_half = old_weight[0].reshape(8 * SLOTS, 2, 2, 3, 128).transpose(2, 0, 3, 1, 4).reshape(2, 8 * SLOTS, 768)
    got = send(of_core(by_half, 0, other=True), "c", 1)
    chip_slots = jnp.concatenate([of_core(by_half, 0), got], axis=0)
    narrow_slots, wide_slots = chip_slots[:, :256], chip_slots[:, 256:]
    wide_slots = chip_merge(gather_axis(wide_slots, "y"))
    wide_slots, tokens, cotangent, old_first, old_second, old_holder, new_owner = lax.optimization_barrier(
        (wide_slots, tokens, cotangent, old_first, old_second, old_holder, new_owner)
    )
    wide_slots = lax.all_gather(wide_slots, ("z", "x"), axis=0, tiled=True).reshape(16, 320, 512)
    narrow_slots = chip_merge(gather_axis(narrow_slots, "x"))
    narrow_slots = gather_axis(plane_merge(gather_axis(narrow_slots, "z")), "y")

    moments = jnp.concatenate([old_first[0].astype(BF16), old_second[0].astype(BF16)], axis=1)
    moments = moments.reshape(4, 2, 2 * SLOTS, 1536)
    chip = jnp.concatenate([of_core(moments, 1), send(of_core(moments, 1, other=True), "c", 1)], axis=1)

    def for_y(shift):
        return lax.dynamic_index_in_dim(chip, (me["y"] + shift) % 4, 0, keepdims=False)

    shard_moments = jnp.concatenate([for_y(0)] + [send(for_y(shift), "y", shift) for shift in SHIFTS], axis=0)

    other_tokens = send(tokens, "c", 1)
    cot_half = cotangent.reshape(512, 2, 384)
    own_cot = of_core(cot_half, 1)
    other_cot = send(of_core(cot_half, 1, other=True), "c", 1)
    pair = jnp.concatenate([tokens, other_tokens], axis=0)

    def gradient(dmixed):
        return lax.dot_general(pair, dmixed, (((0,), (0,)), ((), ())), preferred_element_type=F32).astype(BF16)

    holder = old_holder[:, 0].reshape(8, 512)
    order = jnp.arange(512, dtype=jnp.int32)
    before = order[None, :] < order[:, None]
    held_rank = jnp.sum(((holder[:, None, :] == holder[:, :, None]) & before[None]).astype(jnp.int32), axis=2)
    within = (holder % 2 != core).astype(jnp.int32) * SLOTS + held_rank
    rel = {
        "z": relative(holder // 32, me["z"]),
        "x": relative(holder // 8 % 4, me["x"]),
        "y": relative(holder // 2 % 4, me["y"]),
    }
    narrow_index = rel["y"] * 160 + rel["z"] * 40 + rel["x"] * 10 + within
    wide_index = holder // 8 * 40 + rel["y"] * 10 + within

    my_holder = lax.dynamic_index_in_dim(holder, fsdp_at, 0, keepdims=False)
    my_rank = lax.dynamic_index_in_dim(held_rank, fsdp_at, 0, keepdims=False)
    moment_at = (
        my_holder // 8 * 80
        + relative(my_holder // 2 % 4, me["y"]) * 20
        + (my_holder % 2 != core).astype(jnp.int32) * 10
        + my_rank
    )
    owner = lax.dynamic_index_in_dim(new_owner[:, 0].reshape(8, 512), fsdp_at, 0, keepdims=False)
    own_rank = jnp.sum(((owner[None, :] == owner[:, None]) & before).astype(jnp.int32), axis=1)
    picked = (owner == dp_at)[None, :] & (own_rank[None, :] == jnp.arange(128, dtype=jnp.int32)[:, None])
    own_place = jnp.sum(jnp.where(picked, order[None, :] + 1, 0), axis=1) - 1
    own_at = jnp.sum(jnp.where(picked[:48], moment_at[None, :] + 1, 0), axis=1) - 1
    own_second_at = jnp.where(own_at >= 0, own_at + SLOTS, -1)
    none = jnp.full((32,), -1, jnp.int32)
    moment_index = jnp.concatenate([moment_at, moment_at + SLOTS, own_at, own_second_at, none])[None]
    own_place = own_place[None]

    (wide_slots, wide_index, narrow_index, other_tokens, own_cot, other_cot, pair), narrow_slots, (
        shard_moments,
        moment_index,
        own_place,
    ) = together(
        (wide_slots, wide_index, narrow_index, other_tokens, own_cot, other_cot, pair),
        narrow_slots,
        (shard_moments, moment_index, own_place),
    )
    all_moments = lax.all_gather(shard_moments, ("z", "x"), axis=0, tiled=True)
    weight, dmixed = forward(
        wide_index, narrow_index, tokens, other_tokens, own_cot, other_cot, wide_slots, narrow_slots
    )

    grads = [gradient(dmixed[:, group * 256 : (group + 1) * 256]).reshape(4, 2, 4, 128, 256) for group in range(3)]
    plan = ((0, "y"), (2, "z"), (2, "x"))
    own = [chunk(value, dim, axis, 0) for value, (dim, axis) in zip(grads, plan)]
    towards = jnp.where(core == 0, 1, 3)
    turns = [
        [chunk(value, dim, axis, shift) for value, (dim, axis) in zip(grads, plan)]
        for shift in (2, 4 - towards, towards)
    ]

    def turn(parts, shift):
        return [send_by_core(part, axis, shift) for part, (_, axis) in zip(parts, plan)]

    got_one = turn(turns[0], 1)
    _, (late_dmixed, late_weight) = together(turns[0], (dmixed, weight))
    other_part = back(1, late_dmixed, late_weight)
    got_one, own, turns[1], turns[2], (other_part, late_dmixed, late_weight) = together(
        got_one, own, turns[1], turns[2], (other_part, late_dmixed, late_weight)
    )
    got_two = turn(turns[1], 3)
    partner_part = send(other_part, "c", 1)
    turns[2] = [(part.astype(F32) + got.astype(F32)).astype(BF16) for part, got in zip(turns[2], got_one)]
    shard_weight = lax.dynamic_slice_in_dim(late_weight, me["y"] * 1024, 1024, 0).reshape(2, 512, 768)
    weight_keep = of_core(shard_weight, 0)
    weight_give = of_core(shard_weight, 0, other=True)
    got_two, turns[2], own, (partner_part, weight_keep, weight_give) = together(
        got_two, turns[2], own, (partner_part, weight_keep, weight_give)
    )
    got_three = turn(turns[2], 1)
    sums = [part.astype(F32) + got.astype(F32) for part, got in zip(own, got_two)]
    weight_recv = send(weight_give, "c", 1)
    by_y, by_z, by_x = [(part + got.astype(F32)).astype(BF16) for part, got in zip(sums, got_three)]

    rest = jnp.concatenate([by_z.reshape(4, 2, 128, 256), by_x.reshape(4, 2, 128, 256)], axis=-1)
    parts_y, parts_z = chunks(rest, 0, "y"), chunks(by_y, 1, "z")
    got_y = [send(part, "y", shift) for part, shift in zip(parts_y[1:], SHIFTS)]
    got_z = [send(part, "z", shift) for part, shift in zip(parts_z[1:], SHIFTS)]
    rest = total(parts_y[:1] + got_y)
    by_y = total(parts_z[:1] + got_z)

    value = jnp.concatenate([by_y, rest], axis=-1)
    keep = of_core(value, 0)
    recv = send(of_core(value, 0, other=True), "c", 1)
    low = jnp.where(core == 0, keep, recv)
    high = jnp.where(core == 0, recv, keep)
    wide = jnp.concatenate([low[:, :512], high[:, :512]], axis=1)
    narrow = jnp.concatenate([low[:, 512:], high[:, 512:]], axis=1)
    wide, narrow, partner_part = lax.optimization_barrier((wide, narrow, partner_part))
    wide = symmetric_sum(gather_axis(wide, "x")).astype(BF16)
    narrow = symmetric_sum(gather_axis(narrow, "z")).astype(BF16)
    input_grad = back(0, late_dmixed, late_weight, partner_part)
    wide, narrow, all_moments, input_grad = lax.optimization_barrier((wide, narrow, all_moments, input_grad))
    moment_values = moment_rows(moment_index, all_moments)
    place = jnp.stack([me["z"], me["x"]]).astype(jnp.int32)
    wide, narrow, (moment_values,) = together(gather_axis(wide, "z"), gather_axis(narrow, "x"), (moment_values,))
    summed, square = assemble(place, wide, narrow)
    square = square + send(square, "c", 1)
    square = symmetric_sum(gather_axis(square, "y"))
    new_shard, first_out, second_out = adam(
        core.astype(jnp.int32)[None], square, own_place, summed, moment_values, weight_keep, weight_recv
    )
    return (input_grad, new_shard, first_out[None, None], second_out[None, None])


def solution(mesh):
    chips = Mesh(mesh.devices.reshape(4, 4, 4, 2), ("z", "x", "y", "c"))
    every = ("z", "x", "y", "c")
    placed = (
        P(every, None),
        P(every, None),
        P(every, None, None, None),
        P(every, None, None, None),
        P(every, None, None, None),
        P(),
        P(),
    )
    return jax.shard_map(
        on_device,
        mesh=chips,
        in_specs=placed,
        out_specs=(
            P(every, None),
            P(("y", "c"), None),
            P(("y", "c"), ("z", "x"), None, None),
            P(("y", "c"), ("z", "x"), None, None),
        ),
        check_vma=False,
    )
```

```python
import math

import jax
import jax.numpy as jnp
from jax import lax
from jax.experimental import pallas as pl
from jax.experimental.pallas import tpu as pltpu
from jax.sharding import Mesh
from jax.sharding import PartitionSpec as P

beta_one = 0.9
beta_two = 0.999
learn_rate = 0.01
adam_eps = 1e-08
step_count = 100

SIZE = {"z": 4, "x": 4, "y": 4, "c": 2}
SHIFTS = (1, 3, 2)
OFFSETS = (0, 3, 1, 2)
SLOTS = 5
BF16 = jnp.bfloat16
F32 = jnp.float32


def send(value, axis, shift):
    size = SIZE[axis]
    return lax.ppermute(value, axis, [(i, (i + shift) % size) for i in range(size)])


def send_by_core(value, axis, shift):
    pairs = [(i * 2 + c, (i + (shift if c == 0 else 4 - shift)) % 4 * 2 + c) for i in range(4) for c in range(2)]
    return lax.ppermute(value, (axis, "c"), pairs)


def gather_axis(block, axis):
    return [block] + [send(block, axis, shift) for shift in SHIFTS]


def relative(source, mine):
    away = (source - mine) % 4
    return jnp.where(away == 0, 0, jnp.where(away == 3, 1, jnp.where(away == 1, 2, 3)))


def symmetric_sum(parts):
    own, left, right, across = [part.astype(F32) for part in parts]
    return (own + across) + (left + right)


def pick_rows(index, rows):
    column = jnp.transpose(jnp.broadcast_to(index, (128, index.shape[1])))
    lanes = lax.broadcasted_iota(jnp.int32, column.shape, 1)
    pick = [(column == lanes + at).astype(F32).astype(BF16) for at in range(0, rows.shape[0], 128)]
    return jnp.dot(jnp.concatenate(pick, axis=1), rows, preferred_element_type=F32).astype(BF16)


def params(mib):
    return pltpu.CompilerParams(vmem_limit_bytes=mib * 1024 * 1024)


def cost(macs, moved):
    return pl.CostEstimate(flops=2 * macs, bytes_accessed=moved, transcendentals=0)


def split(i, size):
    return lax.div(i, size), lax.rem(i, size)


def chip_merge_source():
    i = lax.broadcasted_iota(jnp.int32, (1, 384), 1)
    b, rest = split(i, 40)
    chip, rest = split(rest, 10)
    core, k = split(rest, 5)
    return jnp.where(i < 320, chip * 80 + core * 40 + b * 5 + k, -1)


def chip_merge_kernel(a_ref, b_ref, c_ref, d_ref, out_ref, rows_ref):
    for piece, ref in enumerate((a_ref, b_ref, c_ref, d_ref)):
        rows_ref[piece * 80 : (piece + 1) * 80, :] = ref[...]
    rows_ref[320:, :] = jnp.zeros_like(rows_ref[320:, :])
    out_ref[...] = pick_rows(chip_merge_source(), rows_ref[...])[:320]


def chip_merge(parts):
    columns = parts[0].shape[1]
    return pl.pallas_call(
        chip_merge_kernel,
        out_shape=jax.ShapeDtypeStruct((320, columns), BF16),
        scratch_shapes=[pltpu.VMEM((384, columns), BF16)],
        compiler_params=params(16),
        cost_estimate=cost(320 * 320 * columns, 1_000_000),
    )(*parts)


def plane_merge_source():
    i = lax.broadcasted_iota(jnp.int32, (1, 384), 1)
    b, rest = split(i, 160)
    block, j = split(rest, 40)
    return jnp.where(i < 320, block * 80 + b * 40 + j, -1)


def plane_merge_kernel(a_ref, b_ref, c_ref, d_ref, out_ref, rows_ref):
    rows_ref[320:, :] = jnp.zeros_like(rows_ref[320:, :])
    for pair in range(4):
        for piece, ref in enumerate((a_ref, b_ref, c_ref, d_ref)):
            rows_ref[piece * 80 : (piece + 1) * 80, :] = ref[pair * 80 : (pair + 1) * 80, :]
        out_ref[pair * 320 : (pair + 1) * 320, :] = pick_rows(plane_merge_source(), rows_ref[...])[:320]


def plane_merge(parts):
    return pl.pallas_call(
        plane_merge_kernel,
        out_shape=jax.ShapeDtypeStruct((1280, 256), BF16),
        scratch_shapes=[pltpu.VMEM((384, 256), BF16)],
        compiler_params=params(16),
        cost_estimate=cost(4 * 320 * 320 * 256, 1_500_000),
    )(*parts)


def forward_kernel(
    wide_index_ref, narrow_index_ref, own_ref, other_ref, own_cot_ref, other_cot_ref, wide_ref, a_ref, b_ref, c_ref, d_ref,
    weight_ref, dmixed_ref, acc_ref, wide_rows_ref, narrow_rows_ref,
):
    step = pl.program_id(0)

    @pl.when(step == 0)
    def _():
        acc_ref[...] = jnp.zeros_like(acc_ref)

    for b in range(2):
        for chip in range(16):
            wide_rows_ref[b, chip * 40 : (chip + 1) * 40, :] = wide_ref[chip, b * 40 : (b + 1) * 40, :]
        for piece, ref in enumerate((a_ref, b_ref, c_ref, d_ref)):
            narrow_rows_ref[b, piece * 160 : (piece + 1) * 160, :] = ref[b * 160 : (b + 1) * 160, :]
        shard = pl.ds(step * 2 + b, 1)
        rows = slice(b * 512, (b + 1) * 512)
        weight_ref[rows, :256] = pick_rows(narrow_index_ref[shard, :], narrow_rows_ref[b])
        weight_ref[rows, 256:] = pick_rows(wide_index_ref[shard, :], wide_rows_ref[b])
    acc_ref[:512, :] += jnp.dot(own_ref[...], weight_ref[...], preferred_element_type=F32)
    acc_ref[512:, :] += jnp.dot(other_ref[...], weight_ref[...], preferred_element_type=F32)

    @pl.when(step == 3)
    def _():
        for half, cot_ref in enumerate((own_cot_ref, other_cot_ref)):
            for at_row in range(0, 512, 64):
                rows = slice(half * 512 + at_row, half * 512 + at_row + 64)
                for group in range(3):
                    at = group * 256
                    gate = acc_ref[rows, at : at + 128]
                    up = acc_ref[rows, at + 128 : at + 256]
                    cot = cot_ref[at_row : at_row + 64, group * 128 : (group + 1) * 128].astype(F32)
                    sig = 1.0 / (1.0 + jnp.exp(-gate))
                    dmixed_ref[rows, at : at + 128] = (cot * up * sig * (1.0 + gate * (1.0 - sig))).astype(BF16)
                    dmixed_ref[rows, at + 128 : at + 256] = (cot * gate * sig).astype(BF16)


def forward(wide_index, narrow_index, own, other, own_cot, other_cot, wide, narrow):
    index_spec = pl.BlockSpec((8, 512), lambda i: (0, 0))
    tokens_spec = pl.BlockSpec((512, 1024), lambda i: (0, i))
    cot_spec = pl.BlockSpec((512, 384), lambda i: (0, 0))
    return pl.pallas_call(
        forward_kernel,
        grid=(4,),
        in_specs=[index_spec, index_spec, tokens_spec, tokens_spec, cot_spec, cot_spec]
        + [pl.BlockSpec((16, 80, 512), lambda i: (0, i, 0))]
        + [pl.BlockSpec((320, 256), lambda i: (i, 0))] * 4,
        out_specs=[pl.BlockSpec((1024, 768), lambda i: (i, 0)), pl.BlockSpec((1024, 768), lambda i: (0, 0))],
        out_shape=[jax.ShapeDtypeStruct((4096, 768), BF16), jax.ShapeDtypeStruct((1024, 768), BF16)],
        scratch_shapes=[
            pltpu.VMEM((1024, 768), F32),
            pltpu.VMEM((2, 640, 512), BF16),
            pltpu.VMEM((2, 640, 256), BF16),
        ],
        compiler_params=params(50),
        cost_estimate=cost(1024 * 4096 * 768 + 4096 * 640 * 768, 24_000_000),
    )(wide_index, narrow_index, own, other, own_cot, other_cot, wide, *narrow)


def back_kernel(dmixed_ref, weight_ref, *rest):
    total = lax.dot_general(dmixed_ref[...], weight_ref[...], (((1,), (1,)), ((), ())), preferred_element_type=F32)
    if len(rest) == 2:
        total = total + rest[0][...].astype(F32)
    rest[-1][...] = total.astype(BF16)


def back(half, dmixed, weight, add=None):
    out_spec = pl.BlockSpec((512, 512), lambda b: (0, b))
    specs = [pl.BlockSpec((512, 768), lambda b: (half, 0)), pl.BlockSpec((512, 768), lambda b: (b, 0))]
    extra = []
    if add is not None:
        specs.append(out_spec)
        extra.append(add)
    return pl.pallas_call(
        back_kernel,
        grid=(8,),
        in_specs=specs,
        out_specs=out_spec,
        out_shape=jax.ShapeDtypeStruct((512, 4096), BF16),
        compiler_params=params(32),
        cost_estimate=cost(512 * 4096 * 768, 14_000_000),
    )(dmixed, weight, *extra)


def moment_kernel(index_ref, in_ref, out_ref):
    out_ref[...] = pick_rows(index_ref[...], in_ref[...])


def moment_rows(index, gathered):
    count = index.shape[1]
    return pl.pallas_call(
        moment_kernel,
        grid=(3,),
        in_specs=[pl.BlockSpec((1, count), lambda j: (0, 0)), pl.BlockSpec((1280, 512), lambda j: (0, j))],
        out_specs=pl.BlockSpec((count, 512), lambda j: (0, j)),
        out_shape=jax.ShapeDtypeStruct((count, 1536), BF16),
        compiler_params=params(28),
        cost_estimate=cost(count * 1280 * 1536, 8_000_000),
    )(index, gathered)


def assemble_kernel(place_ref, *refs):
    out_ref, square_ref = refs[8], refs[9]
    for which, groups in enumerate(((0, 1), (2,))):
        for ref, offset in zip(refs[which * 4 : which * 4 + 4], OFFSETS):
            rows = pl.ds(pl.multiple_of(((place_ref[which] + offset) % 4) * 128, 128), 128)
            for core in range(2):
                for nth, group in enumerate(groups):
                    for part in range(2):
                        at = core * 256 * len(groups) + nth * 256 + part * 128
                        to = part * 768 + core * 384 + group * 128
                        out_ref[rows, to : to + 128] = ref[:, at : at + 128]
    total = jnp.zeros((8, 128), F32)
    for step in range(16):
        rows = out_ref[step * 32 : (step + 1) * 32, :].astype(F32)
        total = total + jnp.sum((rows * rows).reshape(4, 8, 12, 128), axis=(0, 2))
    square_ref[...] = total


def assemble(place, left, right):
    vmem = pl.BlockSpec(memory_space=pltpu.VMEM)
    return pl.pallas_call(
        assemble_kernel,
        in_specs=[pl.BlockSpec(memory_space=pltpu.SMEM)] + [vmem] * 8,
        out_specs=[vmem, vmem],
        out_shape=[jax.ShapeDtypeStruct((512, 1536), BF16), jax.ShapeDtypeStruct((8, 128), F32)],
        compiler_params=params(16),
        cost_estimate=cost(0, 3_200_000),
    )(place, *left, *right)


def adam_kernel(core_ref, square_ref, place_ref, grad_ref, moments_ref, *refs):
    keep_refs, recv_refs, (new_ref, first_ref, second_ref) = refs[:3], refs[3:6], refs[6:]
    clip_norm = math.sqrt(4096 * 1536)
    factor = jnp.minimum(1.0, clip_norm / jnp.sqrt(jnp.sum(square_ref[...]) + 1e-06))
    bias_one = 1.0 - beta_one**step_count
    bias_two = 1.0 - beta_two**step_count
    kept = pl.program_id(0) % 2 == core_ref[0]

    step_one = learn_rate / bias_one
    to_first = (1.0 - beta_one) * factor
    to_second = (1.0 - beta_two) * factor * factor

    for group in range(3):
        at = slice(group * 128, (group + 1) * 128)
        for at_row in range(0, 512, 64):
            rows = slice(at_row, at_row + 64)
            grad = grad_ref[rows, at].astype(F32)
            first = moments_ref[rows, at].astype(F32) * (beta_one * step_one) + grad * (to_first * step_one)
            second = moments_ref[512 + at_row : 576 + at_row, at].astype(F32) * (beta_two / bias_two)
            second = second + grad * grad * (to_second / bias_two)
            below = second * lax.rsqrt(second) + adam_eps
            guess = pl.reciprocal(below, approx=True)
            update = first * (guess * (2.0 - below * guess))
            weight = jnp.where(kept, keep_refs[group][rows, :], recv_refs[group][rows, :])
            new_ref[rows, at] = (weight.astype(F32) - update).astype(BF16)
    own_grad = pick_rows(place_ref[...], grad_ref[...])[:48].astype(F32)
    filled = jnp.transpose(jnp.broadcast_to(place_ref[...], (128, 128)))[:48, :1] >= 0
    first_own = beta_one * moments_ref[1024:1072, :].astype(F32) + to_first * own_grad
    second_own = beta_two * moments_ref[1072:1120, :].astype(F32) + (1.0 - beta_two) * (factor * own_grad) * (factor * own_grad)
    first_ref[...] = jnp.where(filled, first_own, 0.0)
    second_ref[...] = jnp.where(filled, second_own, 0.0)


def adam(core, square, place, grad, moments, keep, recv):
    wide = pl.BlockSpec((512, 384), lambda j: (0, j))
    own = pl.BlockSpec((48, 384), lambda j: (0, j))
    weight_specs = [pl.BlockSpec((512, 128), lambda j, group=group: (0, group * 2 + j // 2)) for group in range(3)]
    return pl.pallas_call(
        adam_kernel,
        grid=(4,),
        in_specs=[
            pl.BlockSpec(memory_space=pltpu.SMEM),
            pl.BlockSpec((8, 128), lambda j: (0, 0)),
            pl.BlockSpec((1, 128), lambda j: (0, 0)),
            wide,
            pl.BlockSpec((1152, 384), lambda j: (0, j)),
        ]
        + weight_specs * 2,
        out_specs=[wide, own, own],
        out_shape=[
            jax.ShapeDtypeStruct((512, 1536), BF16),
            jax.ShapeDtypeStruct((48, 1536), F32),
            jax.ShapeDtypeStruct((48, 1536), F32),
        ],
        compiler_params=params(24),
        cost_estimate=cost(48 * 512 * 1536, 9_000_000),
    )(core, square, place, grad, moments, keep, keep, keep, recv, recv, recv)


def on_device(tokens, cotangent, old_weight, old_first, old_second, old_holder, new_owner):
    me = {axis: lax.axis_index(axis) for axis in "zxyc"}
    core = me["c"]
    dp_at = me["z"] * 4 + me["x"]
    fsdp_at = me["y"] * 2 + core

    def of_core(value, axis, other=False):
        return lax.dynamic_index_in_dim(value, 1 - core if other else core, axis, keepdims=False)

    def chunk(value, dim, axis, shift):
        return lax.dynamic_index_in_dim(value, (me[axis] + shift) % 4, dim, keepdims=False)

    def chunks(value, dim, axis):
        return [chunk(value, dim, axis, 0)] + [chunk(value, dim, axis, shift) for shift in SHIFTS]

    def together(*groups):
        flat = lax.optimization_barrier(tuple(item for group in groups for item in group))
        out = []
        for group in groups:
            out.append(list(flat[: len(group)]))
            flat = flat[len(group) :]
        return out

    def total(parts):
        return symmetric_sum(parts).astype(BF16)

    by_half = old_weight[0].reshape(8 * SLOTS, 2, 2, 3, 128).transpose(2, 0, 3, 1, 4).reshape(2, 8 * SLOTS, 768)
    got = send(of_core(by_half, 0, other=True), "c", 1)
    chip_slots = jnp.concatenate([of_core(by_half, 0), got], axis=0)
    narrow_slots, wide_slots = chip_slots[:, :256], chip_slots[:, 256:]
    wide_slots = chip_merge(gather_axis(wide_slots, "y"))
    wide_slots, tokens, cotangent, old_first, old_second, old_holder, new_owner = lax.optimization_barrier(
        (wide_slots, tokens, cotangent, old_first, old_second, old_holder, new_owner)
    )
    wide_slots = lax.all_gather(wide_slots, ("z", "x"), axis=0, tiled=True).reshape(16, 320, 512)
    narrow_slots = chip_merge(gather_axis(narrow_slots, "x"))
    narrow_slots = gather_axis(plane_merge(gather_axis(narrow_slots, "z")), "y")

    moments = jnp.concatenate([old_first[0].astype(BF16), old_second[0].astype(BF16)], axis=1)
    moments = moments.reshape(4, 2, 2 * SLOTS, 1536)
    chip = jnp.concatenate([of_core(moments, 1), send(of_core(moments, 1, other=True), "c", 1)], axis=1)

    def for_y(shift):
        return lax.dynamic_index_in_dim(chip, (me["y"] + shift) % 4, 0, keepdims=False)

    shard_moments = jnp.concatenate([for_y(0)] + [send(for_y(shift), "y", shift) for shift in SHIFTS], axis=0)

    other_tokens = send(tokens, "c", 1)
    cot_half = cotangent.reshape(512, 2, 384)
    own_cot = of_core(cot_half, 1)
    other_cot = send(of_core(cot_half, 1, other=True), "c", 1)
    pair = jnp.concatenate([tokens, other_tokens], axis=0)

    def gradient(dmixed):
        return lax.dot_general(pair, dmixed, (((0,), (0,)), ((), ())), preferred_element_type=F32).astype(BF16)

    holder = old_holder[:, 0].reshape(8, 512)
    order = jnp.arange(512, dtype=jnp.int32)
    before = order[None, :] < order[:, None]
    held_rank = jnp.sum(((holder[:, None, :] == holder[:, :, None]) & before[None]).astype(jnp.int32), axis=2)
    within = (holder % 2 != core).astype(jnp.int32) * SLOTS + held_rank
    rel = {
        "z": relative(holder // 32, me["z"]),
        "x": relative(holder // 8 % 4, me["x"]),
        "y": relative(holder // 2 % 4, me["y"]),
    }
    narrow_index = rel["y"] * 160 + rel["z"] * 40 + rel["x"] * 10 + within
    wide_index = holder // 8 * 40 + rel["y"] * 10 + within

    my_holder = lax.dynamic_index_in_dim(holder, fsdp_at, 0, keepdims=False)
    my_rank = lax.dynamic_index_in_dim(held_rank, fsdp_at, 0, keepdims=False)
    moment_at = (
        my_holder // 8 * 80
        + relative(my_holder // 2 % 4, me["y"]) * 20
        + (my_holder % 2 != core).astype(jnp.int32) * 10
        + my_rank
    )
    owner = lax.dynamic_index_in_dim(new_owner[:, 0].reshape(8, 512), fsdp_at, 0, keepdims=False)
    own_rank = jnp.sum(((owner[None, :] == owner[:, None]) & before).astype(jnp.int32), axis=1)
    picked = (owner == dp_at)[None, :] & (own_rank[None, :] == jnp.arange(128, dtype=jnp.int32)[:, None])
    own_place = jnp.sum(jnp.where(picked, order[None, :] + 1, 0), axis=1) - 1
    own_at = jnp.sum(jnp.where(picked[:48], moment_at[None, :] + 1, 0), axis=1) - 1
    own_second_at = jnp.where(own_at >= 0, own_at + SLOTS, -1)
    none = jnp.full((32,), -1, jnp.int32)
    moment_index = jnp.concatenate([moment_at, moment_at + SLOTS, own_at, own_second_at, none])[None]
    own_place = own_place[None]

    (wide_slots, wide_index, narrow_index, other_tokens, own_cot, other_cot, pair), narrow_slots, (
        shard_moments,
        moment_index,
        own_place,
    ) = together(
        (wide_slots, wide_index, narrow_index, other_tokens, own_cot, other_cot, pair),
        narrow_slots,
        (shard_moments, moment_index, own_place),
    )
    all_moments = lax.all_gather(shard_moments, ("z", "x"), axis=0, tiled=True)
    weight, dmixed = forward(
        wide_index, narrow_index, tokens, other_tokens, own_cot, other_cot, wide_slots, narrow_slots
    )

    grads = [gradient(dmixed[:, group * 256 : (group + 1) * 256]).reshape(4, 2, 4, 128, 256) for group in range(3)]
    plan = ((0, "y"), (2, "z"), (2, "x"))
    own = [chunk(value, dim, axis, 0) for value, (dim, axis) in zip(grads, plan)]
    towards = jnp.where(core == 0, 1, 3)
    turns = [
        [chunk(value, dim, axis, shift) for value, (dim, axis) in zip(grads, plan)]
        for shift in (2, 4 - towards, towards)
    ]

    def turn(parts, shift):
        return [send_by_core(part, axis, shift) for part, (_, axis) in zip(parts, plan)]

    got_one = turn(turns[0], 1)
    _, (late_dmixed, late_weight) = together(turns[0], (dmixed, weight))
    other_part = back(1, late_dmixed, late_weight)
    got_one, own, turns[1], turns[2], (other_part, late_dmixed, late_weight) = together(
        got_one, own, turns[1], turns[2], (other_part, late_dmixed, late_weight)
    )
    got_two = turn(turns[1], 3)
    partner_part = send(other_part, "c", 1)
    turns[2] = [(part.astype(F32) + got.astype(F32)).astype(BF16) for part, got in zip(turns[2], got_one)]
    shard_weight = lax.dynamic_slice_in_dim(late_weight, me["y"] * 1024, 1024, 0).reshape(2, 512, 768)
    weight_keep = of_core(shard_weight, 0)
    weight_give = of_core(shard_weight, 0, other=True)
    got_two, turns[2], own, (partner_part, weight_keep, weight_give) = together(
        got_two, turns[2], own, (partner_part, weight_keep, weight_give)
    )
    got_three = turn(turns[2], 1)
    sums = [part.astype(F32) + got.astype(F32) for part, got in zip(own, got_two)]
    weight_recv = send(weight_give, "c", 1)
    by_y, by_z, by_x = [(part + got.astype(F32)).astype(BF16) for part, got in zip(sums, got_three)]

    rest = jnp.concatenate([by_z.reshape(4, 2, 128, 256), by_x.reshape(4, 2, 128, 256)], axis=-1)
    parts_y, parts_z = chunks(rest, 0, "y"), chunks(by_y, 1, "z")
    got_y = [send(part, "y", shift) for part, shift in zip(parts_y[1:], SHIFTS)]
    got_z = [send(part, "z", shift) for part, shift in zip(parts_z[1:], SHIFTS)]
    rest = total(parts_y[:1] + got_y)
    by_y = total(parts_z[:1] + got_z)

    value = jnp.concatenate([by_y, rest], axis=-1)
    keep = of_core(value, 0)
    recv = send(of_core(value, 0, other=True), "c", 1)
    low = jnp.where(core == 0, keep, recv)
    high = jnp.where(core == 0, recv, keep)
    wide = jnp.concatenate([low[:, :512], high[:, :512]], axis=1)
    narrow = jnp.concatenate([low[:, 512:], high[:, 512:]], axis=1)
    wide, narrow, partner_part = lax.optimization_barrier((wide, narrow, partner_part))
    wide = symmetric_sum(gather_axis(wide, "x")).astype(BF16)
    narrow = symmetric_sum(gather_axis(narrow, "z")).astype(BF16)
    input_grad = back(0, late_dmixed, late_weight, partner_part)
    wide, narrow, all_moments, input_grad = lax.optimization_barrier((wide, narrow, all_moments, input_grad))
    moment_values = moment_rows(moment_index, all_moments)
    place = jnp.stack([me["z"], me["x"]]).astype(jnp.int32)
    wide, narrow, (moment_values,) = together(gather_axis(wide, "z"), gather_axis(narrow, "x"), (moment_values,))
    summed, square = assemble(place, wide, narrow)
    square = square + send(square, "c", 1)
    square = symmetric_sum(gather_axis(square, "y"))
    new_shard, first_out, second_out = adam(
        core.astype(jnp.int32)[None], square, own_place, summed, moment_values, weight_keep, weight_recv
    )
    return (input_grad, new_shard, first_out[None, None], second_out[None, None])


def solution(mesh):
    chips = Mesh(mesh.devices.reshape(4, 4, 4, 2), ("z", "x", "y", "c"))
    every = ("z", "x", "y", "c")
    placed = (
        P(every, None),
        P(every, None),
        P(every, None, None, None),
        P(every, None, None, None),
        P(every, None, None, None),
        P(),
        P(),
    )
    return jax.shard_map(
        on_device,
        mesh=chips,
        in_specs=placed,
        out_specs=(
            P(every, None),
            P(("y", "c"), None),
            P(("y", "c"), ("z", "x"), None, None),
            P(("y", "c"), ("z", "x"), None, None),
        ),
        check_vma=False,
    )
```
